256 devices in a mesh: dp: 8 (over x, core), expert: 32 (over z, y).
Axes of the slice: x: 4, y: 4, z: 8, core: 2. Of those that a mesh axis runs over, the one named last changes fastest.
Arguments:
- tokens: bfloat16 [256, 3584], P('expert', 'dp'), may hold values from -6 to 6
- d_out: bfloat16 [256, 3584], P('expert', 'dp'), may hold values from -6 to 6
- gate_dense: bfloat16 [3584, 12288], P('expert', 'dp'), may hold values from -0.09375 to 0.09375
- up_dense: bfloat16 [3584, 12288], P('expert', 'dp'), may hold values from -0.09375 to 0.09375
- down_dense: bfloat16 [12288, 3584], P('dp', 'expert'), may hold values from -0.125 to 0.125
- block_map: int32 [32, 16], replicated, may hold values from 0 to 95, as said below
- routes: int32 [256, 8], P('expert'), may hold values from 0 to 31, all different within a row; in each aligned block of 8 rows (0 to 7, 8 to 15, ...) at most 4 rows name the same one
- route_gates: float32 [8], replicated, may hold values from 0.1 to 1
Outputs:
- mixed: bfloat16 [256, 3584], P('expert', 'dp')
- d_tokens: bfloat16 [256, 3584], P('expert', 'dp')
- gate_dense_grad: float32 [3584, 12288], P('expert', 'dp')
- up_dense_grad: float32 [3584, 12288], P('expert', 'dp')
- down_dense_grad: float32 [12288, 3584], P('dp', 'expert')
The draws below stay inside these ranges and needn't reach their ends.
Inputs may be any that keep to these rules, and one draw needn't show every extreme that they name: `block_map`: for every expert and every j below 8, the entries j * 2 to (j + 1) * 2 - 1 of its row are different blocks of the old shard j, numbered j * 12 to (j + 1) * 12 - 1. Among the 8 tokens of one index of expert, no expert is named by more than 4 routes, and in every draw some expert is named by exactly 4 routes of some such block.
All inputs are finite; a program needn't handle non-finite values.
Results may differ from the reference program's by a relative error of at most 0.019.
Values may be sent and summed in bfloat16 or wider, within the bound.
A program may use at most 128 MiB of HBM per device.

```python
import math
import jax
import jax.numpy as jnp
import numpy as np
from jax import lax

D = 3584
BLK = 128
NB = 96
EB = 16
TOPK = 8
TOK_COL = 8
EXPERTS = 32
CAP = 4
TOKENS = 256
FF = 12288
EFF = 2048
BPD = 2
BLK_DP = 12
N_DP = 8
N_EXPERT = 32


def draw_block_map(key, part):
    key = jax.random.fold_in(key, 7)
    key_list = jax.random.split(key, EXPERTS * N_DP)
    orders = jax.vmap(lambda single: jax.random.permutation(single, BLK_DP))(key_list)
    chosen = orders[:, :BPD].astype(jnp.int32).reshape(EXPERTS, N_DP, BPD)
    offsets = (jnp.arange(N_DP, dtype=jnp.int32) * BLK_DP)[None, :, None]
    return (chosen + offsets).reshape(EXPERTS, EB).astype(jnp.int32)


def levels(rng, shape, shards, least, high):
    gain = 1.0
    for position, parts in shards:
        steps = jax.random.uniform(jax.random.fold_in(jax.random.fold_in(rng, 6), position), (parts,), jnp.float32, least / len(shards), high / len(shards))
        gain = gain * jnp.repeat(jnp.exp(steps), shape[position] // parts).reshape((-1,) + (1,) * (len(shape) - 1 - position))
    return gain


def assign_block(rng, own, number, rows, count, top, bound, slope):
    sequence = jax.random.permutation(rng, count)
    crowded, ordinary = portions_of(count, rows * top, bound, slope, True), portions_of(count, rows * top, bound, slope, False)
    places = jnp.arange(count)

    def named(tallies, turn):
        used = int((tallies > 0).sum())
        fixed = max(1, used // 4)
        passed = fixed + (places - fixed + turn * (used - fixed)) % max(1, count - fixed)
        return jnp.zeros((count,), jnp.int32).at[sequence[jnp.where(places < fixed, places, passed)]].set(jnp.asarray(tallies, jnp.int32))

    tallies = jnp.where(number % 4 == 0, named(crowded, number // 4), named(ordinary, number - number // 4 - 1))
    mixed = jax.random.permutation(jax.random.fold_in(own, 3), count)
    giver, taker = mixed[0:count // 2 * 2:2], mixed[1:count // 2 * 2:2]
    room = jnp.minimum(tallies[giver] - 1, bound - tallies[taker]) // 2
    room = jnp.where((giver == sequence[0]) | (taker == sequence[0]) | (tallies[taker] == 0), 0, jnp.maximum(room, 0))
    passed = jax.random.randint(jax.random.fold_in(own, 4), (count // 2,), 0, 1 << 20) % (room + 1)
    tallies = tallies.at[giver].add(-passed).at[taker].add(passed)
    items = jnp.searchsorted(jnp.cumsum(tallies), jnp.arange(rows * top), side="right").astype(jnp.int32)
    grid = items.reshape(top, rows).T
    grid = grid[jax.random.permutation(jax.random.fold_in(own, 1), rows)]
    turn = jax.random.randint(jax.random.fold_in(own, 2), (rows, 1), 0, top)
    return jnp.take_along_axis(grid, (jnp.arange(top)[None, :] + turn) % top, axis=1)


def portions_of(count, total, reach, lean, full):
    weights = [(1 << 20) // math.isqrt(grade ** lean) + 1 for grade in range(1, count + 1)]
    largest = reach if full else min(reach, max(-(-total // count), total * weights[0] // sum(weights)))
    least = 1 if total - largest >= count - 1 else 0
    holding, spare = [largest] + [least] * (count - 1), total - largest - least * (count - 1)
    while spare > 0:
        free = [i for i in range(1, count) if holding[i] < largest] or [i for i in range(1, count) if holding[i] < reach]
        whole, remaining = sum([weights[i] for i in free]), spare
        for i in free:
            addition = min(reach - holding[i], max(1, remaining * weights[i] // whole), spare)
            holding[i] = holding[i] + addition
            spare = spare - addition
    return np.array(holding)


def noise(rng, shape, scale, most, cuts=(), kind=jnp.bfloat16):
    array = jax.random.normal(rng, shape, jnp.float32) * scale
    if len(cuts) > 0:
        array = levels(rng, shape, cuts, -0.22, 0.18) * array
    return jnp.clip(array, min=-most, max=most).astype(kind)


def setup_inputs(seed: int = 0) -> dict:
    seeds = jax.random.split(jax.random.key(seed), 9)
    tokens = noise(seeds[0], (TOKENS, D), 1.0, 6.0, ((0, 32), (1, 8)))
    d_out = noise(seeds[1], (TOKENS, D), 1.0, 6.0, ((0, 32), (1, 8)))
    gate_dense = noise(seeds[2], (D, FF), D ** -0.5, 0.09375, ((0, 32), (1, 8)))
    up_dense = noise(seeds[3], (D, FF), D ** -0.5, 0.09375, ((0, 32), (1, 8)))
    down_dense = noise(seeds[4], (FF, D), EFF ** -0.5, 0.125, ((0, 8), (1, 32)))
    block_map = draw_block_map(jax.random.fold_in(seeds[8], 71), 0)
    routes_keys = jax.random.split(jax.random.fold_in(seeds[6], 1), TOKENS // TOK_COL)
    routes_turns = jax.random.permutation(jax.random.fold_in(seeds[6], 3), TOKENS // TOK_COL)
    routes = jax.vmap(lambda own, number: assign_block(jax.random.fold_in(seeds[6], 2), own, number, TOK_COL, EXPERTS, TOPK, CAP, 2))(routes_keys, routes_turns).reshape((TOKENS, TOPK))
    route_gates = jnp.clip(jnp.exp(jax.random.uniform(seeds[7], (TOPK,), jnp.float32, math.log(0.1), math.log(1.0))), 0.1, 1.0)
    return dict(tokens=tokens, d_out=d_out, gate_dense=gate_dense, up_dense=up_dense, down_dense=down_dense, block_map=block_map, routes=routes, route_gates=route_gates)


def reference(tokens, d_out, gate_dense, up_dense, down_dense, block_map, routes, route_gates):
    span = TOK_COL * TOPK
    total_routes = TOKENS * TOPK
    flat_routes = routes.reshape(N_EXPERT, span)
    labels = jnp.arange(EXPERTS, dtype=jnp.int32)
    onehot = (flat_routes[:, :, None] == labels[None, None, :]).astype(jnp.int32)
    slot_rank = jnp.sum(jnp.cumsum(onehot, axis=1) * onehot, axis=2) - 1
    column = jnp.arange(N_EXPERT, dtype=jnp.int32)[:, None]
    target_slot = (flat_routes * (N_EXPERT * CAP) + column * CAP + slot_rank).reshape(-1).astype(jnp.int32)
    slot_count = EXPERTS * N_EXPERT * CAP
    route_ids = jnp.arange(total_routes, dtype=jnp.int32)
    slot_route = jnp.full((slot_count,), total_routes, jnp.int32).at[target_slot].set(route_ids)
    slot_token = slot_route // TOPK
    slot_choice = slot_route % TOPK
    slot_gate = jnp.where(slot_route < total_routes, route_gates[slot_choice], jnp.float32(0.0))
    pad_tokens = jnp.concatenate([tokens, jnp.zeros((1, D), tokens.dtype)], axis=0)
    pad_cotan = jnp.concatenate([d_out, jnp.zeros((1, D), d_out.dtype)], axis=0)
    expert_input = pad_tokens[slot_token].reshape(EXPERTS, N_EXPERT * CAP, D)
    expert_cotangent = (slot_gate[:, None] * pad_cotan[slot_token].astype(jnp.float32)).astype(jnp.bfloat16)
    expert_cotangent = expert_cotangent.reshape(EXPERTS, N_EXPERT * CAP, D)

    gate_blocks = gate_dense.reshape(D, NB, BLK)
    up_blocks = up_dense.reshape(D, NB, BLK)
    down_blocks = down_dense.reshape(NB, BLK, D)
    group_width = BPD * BLK
    rows_all = N_EXPERT * CAP

    def one_expert(carry, inputs):
        grad_gate, grad_up, grad_down = carry
        blocks, x_rows, dy_rows = inputs
        w_gate = jnp.take(gate_blocks, blocks, axis=1).reshape(D, EFF)
        w_up = jnp.take(up_blocks, blocks, axis=1).reshape(D, EFF)
        w_down = jnp.take(down_blocks, blocks, axis=0).reshape(EFF, D)
        gate_pre = jnp.dot(x_rows, w_gate, preferred_element_type=jnp.float32)
        up_pre = jnp.dot(x_rows, w_up, preferred_element_type=jnp.float32)
        silu_gate = jax.nn.silu(gate_pre)
        hidden = (silu_gate * up_pre).astype(jnp.bfloat16)
        hidden_grouped = hidden.astype(jnp.float32).reshape(rows_all, N_DP, group_width)
        down_grouped = w_down.astype(jnp.float32).reshape(N_DP, group_width, D)
        out_parts = jnp.einsum("rjf,jfd->jrd", hidden_grouped, down_grouped, precision=lax.Precision.HIGHEST)
        out_parts = lax.optimization_barrier(out_parts.astype(jnp.bfloat16))
        expert_out = jnp.sum(out_parts.astype(jnp.float32), axis=0).astype(jnp.bfloat16)
        hidden_grad = jnp.dot(dy_rows, w_down.T, preferred_element_type=jnp.float32)
        sigma = jax.nn.sigmoid(gate_pre)
        gate_grad = (hidden_grad * up_pre * sigma * (1.0 + gate_pre * (1.0 - sigma))).astype(jnp.bfloat16)
        up_grad = (hidden_grad * silu_gate).astype(jnp.bfloat16)
        gate_grouped = gate_grad.astype(jnp.float32).reshape(rows_all, N_DP, group_width)
        up_grouped = up_grad.astype(jnp.float32).reshape(rows_all, N_DP, group_width)
        wg_grouped = w_gate.astype(jnp.float32).reshape(D, N_DP, group_width)
        wu_grouped = w_up.astype(jnp.float32).reshape(D, N_DP, group_width)
        in_parts = jnp.einsum("rjf,djf->jrd", gate_grouped, wg_grouped, precision=lax.Precision.HIGHEST)
        in_parts = in_parts + jnp.einsum("rjf,djf->jrd", up_grouped, wu_grouped, precision=lax.Precision.HIGHEST)
        in_parts = lax.optimization_barrier(in_parts.astype(jnp.bfloat16))
        expert_in_grad = jnp.sum(in_parts.astype(jnp.float32), axis=0).astype(jnp.bfloat16)
        block_gate = jnp.dot(x_rows.T, gate_grad, preferred_element_type=jnp.float32).astype(jnp.bfloat16)
        block_up = jnp.dot(x_rows.T, up_grad, preferred_element_type=jnp.float32).astype(jnp.bfloat16)
        block_down = jnp.dot(hidden.T, dy_rows, preferred_element_type=jnp.float32).astype(jnp.bfloat16)
        grad_gate = grad_gate.at[:, blocks].add(block_gate.astype(jnp.float32).reshape(D, EB, BLK))
        grad_up = grad_up.at[:, blocks].add(block_up.astype(jnp.float32).reshape(D, EB, BLK))
        grad_down = grad_down.at[blocks].add(block_down.astype(jnp.float32).reshape(EB, BLK, D))
        return (grad_gate, grad_up, grad_down), (expert_out, expert_in_grad)

    start = (jnp.zeros((D, NB, BLK), jnp.float32), jnp.zeros((D, NB, BLK), jnp.float32),
             jnp.zeros((NB, BLK, D), jnp.float32))
    grads, results = lax.scan(one_expert, start, (block_map, expert_input, expert_cotangent))
    expert_out, expert_in_grad = results
    out_routes = expert_out.reshape(slot_count, D)[target_slot].reshape(TOKENS, TOPK, D)
    in_routes = expert_in_grad.reshape(slot_count, D)[target_slot].reshape(TOKENS, TOPK, D)
    mixed = jnp.sum(route_gates[None, :, None] * out_routes.astype(jnp.float32), axis=1).astype(jnp.bfloat16)
    d_tokens = jnp.sum(in_routes.astype(jnp.float32), axis=1).astype(jnp.bfloat16)
    gate_dense_grad = grads[0].reshape(D, FF)
    up_dense_grad = grads[1].reshape(D, FF)
    down_dense_grad = grads[2].reshape(FF, D)
    return (mixed, d_tokens, gate_dense_grad, up_dense_grad, down_dense_grad)
```

```python
import jax
import jax.numpy as jnp
from jax import lax
from jax.sharding import PartitionSpec as P

BLK = 128


def contract(left, right, left_dim, right_dim):
    return lax.dot_general(
        left, right, (((left_dim,), (right_dim,)), ((), ())), preferred_element_type=jnp.float32
    )


def shards(tokens, d_out, gate_dense, up_dense, down_dense, block_map, routes, route_gates):
    dp_count = lax.axis_size("dp")
    ex_count = lax.axis_size("expert")
    dp_index = lax.axis_index("dp")
    experts_all = block_map.shape[0]
    per_group = block_map.shape[1] // dp_count
    width = gate_dense.shape[1]
    blocks = width // BLK
    rows_owned = gate_dense.shape[0]
    tok = routes.shape[0]
    owned_map = lax.dynamic_slice_in_dim(block_map, dp_index * per_group, per_group, 1)
    picks = owned_map - dp_index * blocks
    takes = jnp.sum((picks[:, :, None] == jnp.arange(blocks)[None, None, :]).astype(jnp.float32), axis=1)
    named = (routes[:, :, None] == jnp.arange(experts_all)[None, None, :]).astype(jnp.float32)
    named = jnp.sum(named * route_gates[None, :, None], axis=1)
    weight = jnp.sum(named[:, :, None] * takes[None, :, :], axis=1)
    weight = jnp.repeat(weight, BLK, axis=1)

    both = jnp.concatenate([tokens, d_out], axis=0)
    full = lax.all_gather(both, "dp", axis=1, tiled=True)
    full = full.reshape(2, tok, ex_count, rows_owned).transpose(2, 0, 1, 3)
    cols = lax.all_to_all(full, "expert", split_axis=0, concat_axis=0, tiled=True)
    x = cols[:, 0].reshape(ex_count * tok, rows_owned)
    dy = cols[:, 1].reshape(ex_count * tok, rows_owned)
    part = jnp.concatenate(
        [contract(x, gate_dense, 1, 0), contract(x, up_dense, 1, 0), contract(dy, down_dense, 1, 1)], axis=1
    ).astype(jnp.bfloat16)
    sums = lax.psum_scatter(part, "expert", scatter_dimension=0, tiled=True).astype(jnp.float32)
    gate_pre, up_pre, hidden_grad = sums[:, :width], sums[:, width : 2 * width], sums[:, 2 * width :]
    sigma = jax.nn.sigmoid(gate_pre)
    silu = gate_pre * sigma
    hidden = weight * silu * up_pre
    gate_grad = weight * hidden_grad * up_pre * sigma * (1.0 + gate_pre * (1.0 - sigma))
    up_grad = weight * hidden_grad * silu
    mine = jnp.concatenate([gate_grad, up_grad, hidden], axis=1).astype(jnp.bfloat16)
    every = lax.all_gather(mine, "expert", axis=0, tiled=True)
    gate_grad, up_grad, hidden = every[:, :width], every[:, width : 2 * width], every[:, 2 * width :]
    gate_dense_grad = contract(x, gate_grad, 0, 0)
    up_dense_grad = contract(x, up_grad, 0, 0)
    down_dense_grad = contract(hidden, dy, 0, 0)
    out_part = contract(hidden, down_dense, 1, 0).astype(jnp.bfloat16)
    in_part = (contract(gate_grad, gate_dense, 1, 1) + contract(up_grad, up_dense, 1, 1)).astype(jnp.bfloat16)
    pair = jnp.stack([out_part.reshape(ex_count, tok, rows_owned), in_part.reshape(ex_count, tok, rows_owned)], axis=1)
    back = lax.all_to_all(pair, "expert", split_axis=0, concat_axis=0, tiled=True)
    back = back.transpose(1, 2, 0, 3).reshape(2 * tok, ex_count * rows_owned)
    done = lax.psum_scatter(back, "dp", scatter_dimension=1, tiled=True)
    return (done[:tok], done[tok:], gate_dense_grad, up_dense_grad, down_dense_grad)


def solution(mesh):
    in_specs = (
        P("expert", "dp"),
        P("expert", "dp"),
        P("expert", "dp"),
        P("expert", "dp"),
        P("dp", "expert"),
        P(),
        P("expert", None),
        P(),
    )
    out_specs = (
        P("expert", "dp"),
        P("expert", "dp"),
        P("expert", "dp"),
        P("expert", "dp"),
        P("dp", "expert"),
    )
    return jax.shard_map(shards, mesh=mesh, in_specs=in_specs, out_specs=out_specs, check_vma=False)
```

```python
import functools

import jax
import jax.numpy as jnp
from jax import lax
from jax.experimental import pallas as pl
from jax.experimental.pallas import tpu as pltpu
from jax.sharding import PartitionSpec as P

BLK = 128
MESH = pl.DeviceIdType.MESH


def contract(left, right, left_dim, right_dim):
    return lax.dot_general(
        left, right, (((left_dim,), (right_dim,)), ((), ())), preferred_element_type=jnp.float32
    )


def kernel(
    nj, ny, nc,
    tok_ref, cot_ref, gate_ref, up_ref, down_ref, wt_ref,
    mixed_ref, dtok_ref, gate_out, up_out, down_out,
    xs, xt, xb, wbuf, wgu, wd, wdf, rs_send, rs_recv, ag, gu_send, d_send, acc, op_send, op_recv, t_send, t_recv,
    xt_ss, xt_rs, wt_ss, wt_rs, xb_ss, xb_rs, w_ss, w_rs, r_ss, r_rs, a_ss, a_rs, g_ss, g_rs, o_ss, o_rs, t_ss, t_rs,
):
    nz = nj
    j = lax.axis_index("dp")
    e = lax.axis_index("expert")
    z, y = e // ny, lax.rem(e, ny)
    rows = gate_ref.shape[0]
    quarter = gate_ref.shape[1] // ny
    group = 8 * ny

    def at_y(k):
        return (j, z * ny + k)

    def at_z(k):
        return (j, k * ny + y)

    def at_j(k):
        return (k, e)

    def at_t(k):
        return (z, j * ny + k)

    def others(n, me, body):
        def step(i, _):
            body(lax.rem(me + i, n))
            return 0

        lax.fori_loop(1, n, step, 0)

    def crossing(body, own):
        def step(k, _):
            same = jnp.logical_and(z == j, k == y)

            @pl.when(jnp.logical_not(same))
            def _():
                body(k)

            if own is not None:
                @pl.when(same)
                def _():
                    own(k)

            return 0

        lax.fori_loop(0, ny, step, 0)

    def remote(src, dst, ss, rs, device):
        return pltpu.make_async_remote_copy(
            src_ref=src, dst_ref=dst, send_sem=ss, recv_sem=rs, device_id=device, device_id_type=MESH
        )

    barrier = pltpu.get_barrier_semaphore()

    def greet(device):
        pl.semaphore_signal(barrier, inc=1, device_id=device, device_id_type=MESH)

    others(ny, y, lambda k: greet(at_y(k)))
    others(nz, z, lambda k: greet(at_z(k)))
    others(nj, j, lambda k: greet(at_j(k)))
    count = (ny - 1) + (nz - 1) + (nj - 1)

    @pl.when(z != j)
    def _():
        def step(k, _):
            greet(at_t(k))
            return 0

        lax.fori_loop(0, ny, step, 0)
        pl.semaphore_wait(barrier, count + ny)

    @pl.when(z == j)
    def _():
        pl.semaphore_wait(barrier, count)

    xs[...] = jnp.concatenate(
        [tok_ref[...].astype(jnp.float32), cot_ref[...].astype(jnp.float32)], axis=0
    ).astype(jnp.bfloat16)

    def x_copy(k):
        return remote(xs, xt.at[y], xt_ss.at[k], xt_rs.at[y], at_t(k))

    def x_wait(k):
        return remote(xs, xt.at[k], xt_ss.at[k], xt_rs.at[k], at_t(k))

    def x_own(k):
        xt[k] = xs[...]

    crossing(lambda k: x_copy(k).start(), x_own)

    def wt_copy(k):
        return remote(wt_ref.at[k], wbuf.at[y], wt_ss.at[k], wt_rs.at[y], at_y(k))

    def wt_wait(k):
        return remote(wt_ref.at[k], wbuf.at[k], wt_ss.at[k], wt_rs.at[k], at_y(k))

    others(ny, y, lambda k: wt_copy(k).start())
    wbuf[y] = wt_ref[y]

    def columns(k, c):
        return pl.ds(pl.multiple_of(k * quarter + c * BLK, BLK), BLK)

    def band(k):
        return pl.ds(pl.multiple_of(k * rows, 16), rows)

    def w_copies(k, c, slot):
        return (
            remote(gate_ref.at[:, columns(k, c)], wgu.at[c, band(slot), pl.ds(0, BLK)],
                   w_ss.at[c, 0, k], w_rs.at[c, 0, slot], at_y(k)),
            remote(up_ref.at[:, columns(k, c)], wgu.at[c, band(slot), pl.ds(BLK, BLK)],
                   w_ss.at[c, 1, k], w_rs.at[c, 1, slot], at_y(k)),
            remote(down_ref.at[columns(k, c), :], wd.at[c, slot],
                   w_ss.at[c, 2, k], w_rs.at[c, 2, slot], at_y(k)),
        )

    def start_all(copies):
        for copy in copies:
            copy.start()

    def recv_all(copies):
        for copy in copies:
            copy.wait_recv()

    def send_all(copies):
        for copy in copies:
            copy.wait_send()

    for c in range(nc):
        others(ny, y, lambda k: start_all(w_copies(k, c, y)))
    for c in range(nc):
        wgu[c, band(y), 0:BLK] = gate_ref[:, columns(y, c)]
        wgu[c, band(y), BLK : 2 * BLK] = up_ref[:, columns(y, c)]
        wd[c, y] = down_ref[columns(y, c), :]

    crossing(lambda k: x_wait(k).wait_recv(), None)
    landed = xt[...].astype(jnp.float32)
    xb[j, 0] = landed[:, :8].reshape(group, -1).astype(jnp.bfloat16)
    xb[j, 1] = landed[:, 8:].reshape(group, -1).astype(jnp.bfloat16)

    def xb_copy(k, slot):
        return remote(xb.at[slot], xb.at[slot], xb_ss.at[k], xb_rs.at[slot], at_j(k))

    others(nj, j, lambda k: xb_copy(k, j).start())
    others(nj, j, lambda k: xb_copy(k, k).wait_recv())
    tokens_all = nj * group
    feats = xb.shape[3]
    x = xb[:, 0].reshape(tokens_all, feats)
    dy = xb[:, 1].reshape(tokens_all, feats)

    def rs_copy(k, c, slot):
        return remote(rs_send.at[c, k], rs_recv.at[c, slot], r_ss.at[c, k], r_rs.at[c, slot], at_z(k))

    for c in range(nc):
        others(ny, y, lambda k: recv_all(w_copies(k, c, k)))
        wdf[c] = jnp.concatenate([wd[c, k] for k in range(ny)], axis=1)
        pre = contract(x, wgu[c], 1, 0)
        hid = contract(dy, wdf[c], 1, 1)
        rs_send[c, :, :, 0 : 2 * BLK] = pre.reshape(nz, group, 2 * BLK).astype(jnp.bfloat16)
        rs_send[c, :, :, 2 * BLK : 3 * BLK] = hid.reshape(nz, group, BLK).astype(jnp.bfloat16)
        others(nz, z, lambda k: rs_copy(k, c, z).start())
        rs_recv[c, z] = rs_send[c, z]

    others(ny, y, lambda k: wt_wait(k).wait_recv())

    def ag_copy(k, c, slot):
        return remote(ag.at[c, slot], ag.at[c, slot], a_ss.at[c, k], a_rs.at[c, slot], at_z(k))

    for c in range(nc):
        others(nz, z, lambda k: rs_copy(k, c, k).wait_recv())
        total = jnp.sum(rs_recv[c].astype(jnp.float32), axis=0)
        gate_pre, up_pre, hidden_grad = total[:, :BLK], total[:, BLK : 2 * BLK], total[:, 2 * BLK :]
        weight = wbuf[:, :, c * BLK : (c + 1) * BLK].reshape(group, BLK)
        sigma = jax.nn.sigmoid(gate_pre)
        silu = gate_pre * sigma
        scaled = weight * hidden_grad
        ag[c, z, :, 0:BLK] = (scaled * up_pre * sigma * (1.0 + gate_pre * (1.0 - sigma))).astype(jnp.bfloat16)
        ag[c, z, :, BLK : 2 * BLK] = (scaled * silu).astype(jnp.bfloat16)
        ag[c, z, :, 2 * BLK : 3 * BLK] = (weight * silu * up_pre).astype(jnp.bfloat16)
        others(nz, z, lambda k: ag_copy(k, c, z).start())

    def g_copies(k, c, slot):
        return (
            remote(gu_send.at[c, band(k), pl.ds(0, BLK)], gate_out.at[:, columns(slot, c)],
                   g_ss.at[c, 0, k], g_rs.at[c, 0, slot], at_y(k)),
            remote(gu_send.at[c, band(k), pl.ds(BLK, BLK)], up_out.at[:, columns(slot, c)],
                   g_ss.at[c, 1, k], g_rs.at[c, 1, slot], at_y(k)),
            remote(d_send.at[c, k], down_out.at[columns(slot, c), :],
                   g_ss.at[c, 2, k], g_rs.at[c, 2, slot], at_y(k)),
        )

    for c in range(nc):
        others(nz, z, lambda k: ag_copy(k, c, k).wait_recv())
        pair = ag[c, :, :, 0 : 2 * BLK].reshape(tokens_all, 2 * BLK)
        hidden = ag[c, :, :, 2 * BLK : 3 * BLK].reshape(tokens_all, BLK)
        gu_send[c] = contract(x, pair, 0, 0).astype(jnp.bfloat16)
        down_part = contract(hidden, dy, 0, 0).astype(jnp.bfloat16)
        for k in range(ny):
            d_send[c, k] = down_part[:, k * rows : (k + 1) * rows]
        others(ny, y, lambda k: start_all(g_copies(k, c, y)))
        out_part = contract(hidden, wdf[c], 1, 0)
        in_part = contract(pair, wgu[c], 1, 1)
        if c == 0:
            acc[0], acc[1] = out_part, in_part
        else:
            acc[0] += out_part
            acc[1] += in_part
    op_send[:, 0] = acc[0].reshape(nj, group, feats).astype(jnp.bfloat16)
    op_send[:, 1] = acc[1].reshape(nj, group, feats).astype(jnp.bfloat16)

    def op_copy(k, slot):
        return remote(op_send.at[k], op_recv.at[slot], o_ss.at[k], o_rs.at[slot], at_j(k))

    others(nj, j, lambda k: op_copy(k, j).start())
    op_recv[j] = op_send[j]
    for c in range(nc):
        gate_out[:, columns(y, c)] = gu_send[c, band(y), 0:BLK]
        up_out[:, columns(y, c)] = gu_send[c, band(y), BLK : 2 * BLK]
        down_out[columns(y, c), :] = d_send[c, y]
    others(nj, j, lambda k: op_copy(k, k).wait_recv())
    summed = jnp.sum(op_recv[...].astype(jnp.float32), axis=0).reshape(2, ny, 8, feats)
    t_send[...] = jnp.concatenate([summed[0], summed[1]], axis=1).astype(jnp.bfloat16)

    def t_copy(k):
        return remote(t_send.at[k], t_recv.at[y], t_ss.at[k], t_rs.at[y], at_t(k))

    def t_wait(k):
        return remote(t_send.at[k], t_recv.at[k], t_ss.at[k], t_rs.at[k], at_t(k))

    def t_own(k):
        t_recv[k] = t_send[k]

    crossing(lambda k: t_copy(k).start(), t_own)
    crossing(lambda k: t_wait(k).wait_recv(), None)
    final = jnp.sum(t_recv[...].astype(jnp.float32), axis=0)
    mixed_ref[...] = final[:8].astype(jnp.bfloat16)
    dtok_ref[...] = final[8:].astype(jnp.bfloat16)

    for c in range(nc):
        others(ny, y, lambda k: recv_all(g_copies(k, c, k)))
    crossing(lambda k: x_copy(k).wait_send(), None)
    crossing(lambda k: t_copy(k).wait_send(), None)
    others(ny, y, lambda k: wt_copy(k).wait_send())
    others(nj, j, lambda k: xb_copy(k, j).wait_send())
    others(nj, j, lambda k: op_copy(k, j).wait_send())
    for c in range(nc):
        others(ny, y, lambda k: send_all(w_copies(k, c, y)))
        others(nz, z, lambda k: rs_copy(k, c, z).wait_send())
        others(nz, z, lambda k: ag_copy(k, c, z).wait_send())
        others(ny, y, lambda k: send_all(g_copies(k, c, y)))


def shards(tokens, d_out, gate_dense, up_dense, down_dense, block_map, routes, route_gates):
    nj = lax.axis_size("dp")
    ny = lax.axis_size("expert") // nj
    dp_index = lax.axis_index("dp")
    experts_all = block_map.shape[0]
    per_group = block_map.shape[1] // nj
    rows, width = gate_dense.shape
    blocks = width // BLK
    tok, feats = tokens.shape
    nc = blocks // ny
    group = tok * ny
    owned_map = lax.dynamic_slice_in_dim(block_map, dp_index * per_group, per_group, 1)
    picks = owned_map - dp_index * blocks
    takes = jnp.sum((picks[:, :, None] == jnp.arange(blocks)[None, None, :]).astype(jnp.float32), axis=1)
    named = (routes[:, :, None] == jnp.arange(experts_all)[None, None, :]).astype(jnp.float32)
    named = jnp.sum(named * route_gates[None, :, None], axis=1)
    weight = jnp.sum(named[:, :, None] * takes[None, :, :], axis=1)
    weight = weight.reshape(tok, ny, nc).transpose(1, 0, 2)
    weight = jnp.broadcast_to(weight[:, :, :, None], (ny, tok, nc, BLK)).reshape(ny, tok, nc * BLK)

    half, full = jnp.bfloat16, jnp.float32
    dma = pltpu.SemaphoreType.DMA
    vmem = pl.BlockSpec(memory_space=pltpu.VMEM)
    mixed, d_tokens, gate_grad, up_grad, down_grad = pl.pallas_call(
        functools.partial(kernel, nj, ny, nc),
        out_shape=(
            jax.ShapeDtypeStruct((tok, feats), half),
            jax.ShapeDtypeStruct((tok, feats), half),
            jax.ShapeDtypeStruct((rows, width), half),
            jax.ShapeDtypeStruct((rows, width), half),
            jax.ShapeDtypeStruct((width, rows), half),
        ),
        in_specs=[vmem] * 6,
        out_specs=(vmem,) * 5,
        scratch_shapes=[
            pltpu.VMEM((2 * tok, feats), half),
            pltpu.VMEM((ny, 2 * tok, feats), half),
            pltpu.VMEM((nj, 2, group, feats), half),
            pltpu.VMEM((ny, tok, nc * BLK), full),
            pltpu.VMEM((nc, ny * rows, 2 * BLK), half),
            pltpu.VMEM((nc, ny, BLK, rows), half),
            pltpu.VMEM((nc, BLK, ny * rows), half),
            pltpu.VMEM((nc, nj, group, 3 * BLK), half),
            pltpu.VMEM((nc, nj, group, 3 * BLK), half),
            pltpu.VMEM((nc, nj, group, 3 * BLK), half),
            pltpu.VMEM((nc, ny * rows, 2 * BLK), half),
            pltpu.VMEM((nc, ny, BLK, rows), half),
            pltpu.VMEM((2, nj * group, feats), full),
            pltpu.VMEM((nj, 2, group, feats), half),
            pltpu.VMEM((nj, 2, group, feats), half),
            pltpu.VMEM((ny, 2 * tok, feats), half),
            pltpu.VMEM((ny, 2 * tok, feats), half),
            dma((ny,)), dma((ny,)), dma((ny,)), dma((ny,)),
            dma((nj,)), dma((nj,)),
            dma((nc, 3, ny)), dma((nc, 3, ny)),
            dma((nc, nj)), dma((nc, nj)), dma((nc, nj)), dma((nc, nj)),
            dma((nc, 3, ny)), dma((nc, 3, ny)),
            dma((nj,)), dma((nj,)), dma((ny,)), dma((ny,)),
        ],
        compiler_params=pltpu.CompilerParams(
            collective_id=0, has_side_effects=True, vmem_limit_bytes=40 * 1024 * 1024
        ),
    )(tokens, d_out, gate_dense, up_dense, down_dense, weight)
    return (
        mixed,
        d_tokens,
        gate_grad.astype(jnp.float32),
        up_grad.astype(jnp.float32),
        down_grad.astype(jnp.float32),
    )


def solution(mesh):
    in_specs = (
        P("expert", "dp"),
        P("expert", "dp"),
        P("expert", "dp"),
        P("expert", "dp"),
        P("dp", "expert"),
        P(),
        P("expert", None),
        P(),
    )
    out_specs = (
        P("expert", "dp"),
        P("expert", "dp"),
        P("expert", "dp"),
        P("expert", "dp"),
        P("dp", "expert"),
    )
    return jax.shard_map(shards, mesh=mesh, in_specs=in_specs, out_specs=out_specs, check_vma=False)
```

```python
import functools

import jax
import jax.numpy as jnp
from jax import lax
from jax.experimental import pallas as pl
from jax.experimental.pallas import tpu as pltpu
from jax.sharding import PartitionSpec as P

BLK = 128
MESH = pl.DeviceIdType.MESH


def contract(left, right, left_dim, right_dim):
    return lax.dot_general(
        left, right, (((left_dim,), (right_dim,)), ((), ())), preferred_element_type=jnp.float32
    )


def kernel(
    nj, ny, nc,
    tok_ref, cot_ref, gate_ref, up_ref, down_ref, wt_ref,
    mixed_ref, dtok_ref, gate_out, up_out, down_out,
    xs, xt, xb, wbuf, wall, rs_send, rs_recv, ag, grads, acc, op_send, op_recv, t_send, t_recv,
    xt_ss, xt_rs, wt_ss, wt_rs, xb_ss, xb_rs, w_ss, w_rs, r_ss, r_rs, a_ss, a_rs, g_ss, g_rs, o_ss, o_rs, t_ss, t_rs,
):
    nz = nj
    j = lax.axis_index("dp")
    e = lax.axis_index("expert")
    z, y = e // ny, lax.rem(e, ny)
    rows = gate_ref.shape[0]
    quarter = gate_ref.shape[1] // ny
    group = 8 * ny

    def at_y(k):
        return (j, z * ny + k)

    def at_z(k):
        return (j, k * ny + y)

    def at_j(k):
        return (k, e)

    def at_t(k):
        return (z, j * ny + k)

    def others(n, me, body):
        def step(i, _):
            body(lax.rem(me + i, n))
            return 0

        lax.fori_loop(1, n, step, 0)

    def crossing(body, own):
        def step(k, _):
            same = jnp.logical_and(z == j, k == y)

            @pl.when(jnp.logical_not(same))
            def _():
                body(k)

            if own is not None:
                @pl.when(same)
                def _():
                    own(k)

            return 0

        lax.fori_loop(0, ny, step, 0)

    def remote(src, dst, ss, rs, device):
        return pltpu.make_async_remote_copy(
            src_ref=src, dst_ref=dst, send_sem=ss, recv_sem=rs, device_id=device, device_id_type=MESH
        )

    barrier = pltpu.get_barrier_semaphore()

    def greet(device):
        pl.semaphore_signal(barrier, inc=1, device_id=device, device_id_type=MESH)

    others(ny, y, lambda k: greet(at_y(k)))
    others(nz, z, lambda k: greet(at_z(k)))
    others(nj, j, lambda k: greet(at_j(k)))
    count = (ny - 1) + (nz - 1) + (nj - 1)

    @pl.when(z != j)
    def _():
        def step(k, _):
            greet(at_t(k))
            return 0

        lax.fori_loop(0, ny, step, 0)
        pl.semaphore_wait(barrier, count + ny)

    @pl.when(z == j)
    def _():
        pl.semaphore_wait(barrier, count)

    xs[...] = jnp.concatenate(
        [tok_ref[...].astype(jnp.float32), cot_ref[...].astype(jnp.float32)], axis=0
    ).astype(jnp.bfloat16)

    def x_copy(k):
        return remote(xs, xt.at[y], xt_ss.at[k], xt_rs.at[y], at_t(k))

    def x_wait(k):
        return remote(xs, xt.at[k], xt_ss.at[k], xt_rs.at[k], at_t(k))

    def x_own(k):
        xt[k] = xs[...]

    crossing(lambda k: x_copy(k).start(), x_own)

    def wt_copy(k):
        return remote(wt_ref.at[k], wbuf.at[y], wt_ss.at[k], wt_rs.at[y], at_y(k))

    def wt_wait(k):
        return remote(wt_ref.at[k], wbuf.at[k], wt_ss.at[k], wt_rs.at[k], at_y(k))

    others(ny, y, lambda k: wt_copy(k).start())
    wbuf[y] = wt_ref[y]

    def columns(k, c):
        return pl.ds(pl.multiple_of(k * quarter + c * BLK, BLK), BLK)

    def band(k):
        return pl.ds(pl.multiple_of(k * rows, 16), rows)

    def w_copies(k, c, slot):
        return (
            remote(gate_ref.at[:, columns(k, c)], wall.at[c, band(slot), pl.ds(0, BLK)],
                   w_ss.at[c, 0, k], w_rs.at[c, 0, slot], at_y(k)),
            remote(up_ref.at[:, columns(k, c)], wall.at[c, band(slot), pl.ds(BLK, BLK)],
                   w_ss.at[c, 1, k], w_rs.at[c, 1, slot], at_y(k)),
            remote(down_ref.at[:, columns(k, c)], wall.at[c, band(slot), pl.ds(2 * BLK, BLK)],
                   w_ss.at[c, 2, k], w_rs.at[c, 2, slot], at_y(k)),
        )

    def start_all(copies):
        for copy in copies:
            copy.start()

    def recv_all(copies):
        for copy in copies:
            copy.wait_recv()

    def send_all(copies):
        for copy in copies:
            copy.wait_send()

    for c in range(nc):
        others(ny, y, lambda k: start_all(w_copies(k, c, y)))
    for c in range(nc):
        wall[c, band(y), 0:BLK] = gate_ref[:, columns(y, c)]
        wall[c, band(y), BLK : 2 * BLK] = up_ref[:, columns(y, c)]
        wall[c, band(y), 2 * BLK : 3 * BLK] = down_ref[:, columns(y, c)]

    crossing(lambda k: x_wait(k).wait_recv(), None)
    landed = xt[...].astype(jnp.float32)
    xb[j, 0] = landed[:, :8].reshape(group, -1).astype(jnp.bfloat16)
    xb[j, 1] = landed[:, 8:].reshape(group, -1).astype(jnp.bfloat16)

    def xb_copy(k, slot):
        return remote(xb.at[slot], xb.at[slot], xb_ss.at[k], xb_rs.at[slot], at_j(k))

    others(nj, j, lambda k: xb_copy(k, j).start())
    others(nj, j, lambda k: xb_copy(k, k).wait_recv())
    tokens_all = nj * group
    feats = xb.shape[3]
    x = xb[:, 0].reshape(tokens_all, feats)
    dy = xb[:, 1].reshape(tokens_all, feats)

    def rs_copy(k, c, slot):
        return remote(rs_send.at[c, k], rs_recv.at[c, slot], r_ss.at[c, k], r_rs.at[c, slot], at_z(k))

    for c in range(nc):
        others(ny, y, lambda k: recv_all(w_copies(k, c, k)))
        pre = contract(x, wall[c, :, 0 : 2 * BLK], 1, 0)
        hid = contract(dy, wall[c, :, 2 * BLK : 3 * BLK], 1, 0)
        rs_send[c, :, :, 0 : 2 * BLK] = pre.reshape(nz, group, 2 * BLK).astype(jnp.bfloat16)
        rs_send[c, :, :, 2 * BLK : 3 * BLK] = hid.reshape(nz, group, BLK).astype(jnp.bfloat16)
        others(nz, z, lambda k: rs_copy(k, c, z).start())
        rs_recv[c, z] = rs_send[c, z]

    others(ny, y, lambda k: wt_wait(k).wait_recv())

    def ag_copy(k, c, slot):
        return remote(ag.at[c, slot], ag.at[c, slot], a_ss.at[c, k], a_rs.at[c, slot], at_z(k))

    for c in range(nc):
        others(nz, z, lambda k: rs_copy(k, c, k).wait_recv())
        total = jnp.sum(rs_recv[c].astype(jnp.float32), axis=0)
        gate_pre, up_pre, hidden_grad = total[:, :BLK], total[:, BLK : 2 * BLK], total[:, 2 * BLK :]
        weight = wbuf[:, :, c * BLK : (c + 1) * BLK].reshape(group, BLK)
        sigma = jax.nn.sigmoid(gate_pre)
        silu = gate_pre * sigma
        scaled = weight * hidden_grad
        ag[c, z, :, 0:BLK] = (scaled * up_pre * sigma * (1.0 + gate_pre * (1.0 - sigma))).astype(jnp.bfloat16)
        ag[c, z, :, BLK : 2 * BLK] = (scaled * silu).astype(jnp.bfloat16)
        ag[c, z, :, 2 * BLK : 3 * BLK] = (weight * silu * up_pre).astype(jnp.bfloat16)
        others(nz, z, lambda k: ag_copy(k, c, z).start())

    def g_copies(k, c, slot):
        return (
            remote(grads.at[c, band(k), pl.ds(0, BLK)], gate_out.at[:, columns(slot, c)],
                   g_ss.at[c, 0, k], g_rs.at[c, 0, slot], at_y(k)),
            remote(grads.at[c, band(k), pl.ds(BLK, BLK)], up_out.at[:, columns(slot, c)],
                   g_ss.at[c, 1, k], g_rs.at[c, 1, slot], at_y(k)),
            remote(grads.at[c, band(k), pl.ds(2 * BLK, BLK)], down_out.at[:, columns(slot, c)],
                   g_ss.at[c, 2, k], g_rs.at[c, 2, slot], at_y(k)),
        )

    for c in range(nc):
        others(nz, z, lambda k: ag_copy(k, c, k).wait_recv())
        pair = ag[c, :, :, 0 : 2 * BLK].reshape(tokens_all, 2 * BLK)
        hidden = ag[c, :, :, 2 * BLK : 3 * BLK].reshape(tokens_all, BLK)
        grads[c, :, 0 : 2 * BLK] = contract(x, pair, 0, 0).astype(jnp.bfloat16)
        grads[c, :, 2 * BLK : 3 * BLK] = contract(dy, hidden, 0, 0).astype(jnp.bfloat16)
        others(ny, y, lambda k: start_all(g_copies(k, c, y)))
        out_part = contract(hidden, wall[c, :, 2 * BLK : 3 * BLK], 1, 1)
        in_part = contract(pair, wall[c, :, 0 : 2 * BLK], 1, 1)
        if c == 0:
            acc[0], acc[1] = out_part, in_part
        else:
            acc[0] += out_part
            acc[1] += in_part
    op_send[:, 0] = acc[0].reshape(nj, group, feats).astype(jnp.bfloat16)
    op_send[:, 1] = acc[1].reshape(nj, group, feats).astype(jnp.bfloat16)

    def op_copy(k, slot):
        return remote(op_send.at[k], op_recv.at[slot], o_ss.at[k], o_rs.at[slot], at_j(k))

    others(nj, j, lambda k: op_copy(k, j).start())
    op_recv[j] = op_send[j]
    for c in range(nc):
        gate_out[:, columns(y, c)] = grads[c, band(y), 0:BLK]
        up_out[:, columns(y, c)] = grads[c, band(y), BLK : 2 * BLK]
        down_out[:, columns(y, c)] = grads[c, band(y), 2 * BLK : 3 * BLK]
    others(nj, j, lambda k: op_copy(k, k).wait_recv())
    summed = jnp.sum(op_recv[...].astype(jnp.float32), axis=0).reshape(2, ny, 8, feats)
    t_send[...] = jnp.concatenate([summed[0], summed[1]], axis=1).astype(jnp.bfloat16)

    def t_copy(k):
        return remote(t_send.at[k], t_recv.at[y], t_ss.at[k], t_rs.at[y], at_t(k))

    def t_wait(k):
        return remote(t_send.at[k], t_recv.at[k], t_ss.at[k], t_rs.at[k], at_t(k))

    def t_own(k):
        t_recv[k] = t_send[k]

    crossing(lambda k: t_copy(k).start(), t_own)
    crossing(lambda k: t_wait(k).wait_recv(), None)
    final = jnp.sum(t_recv[...].astype(jnp.float32), axis=0)
    mixed_ref[...] = final[:8].astype(jnp.bfloat16)
    dtok_ref[...] = final[8:].astype(jnp.bfloat16)

    for c in range(nc):
        others(ny, y, lambda k: recv_all(g_copies(k, c, k)))
    crossing(lambda k: x_copy(k).wait_send(), None)
    crossing(lambda k: t_copy(k).wait_send(), None)
    others(ny, y, lambda k: wt_copy(k).wait_send())
    others(nj, j, lambda k: xb_copy(k, j).wait_send())
    others(nj, j, lambda k: op_copy(k, j).wait_send())
    for c in range(nc):
        others(ny, y, lambda k: send_all(w_copies(k, c, y)))
        others(nz, z, lambda k: rs_copy(k, c, z).wait_send())
        others(nz, z, lambda k: ag_copy(k, c, z).wait_send())
        others(ny, y, lambda k: send_all(g_copies(k, c, y)))


def shards(tokens, d_out, gate_dense, up_dense, down_dense, block_map, routes, route_gates):
    nj = lax.axis_size("dp")
    ny = lax.axis_size("expert") // nj
    dp_index = lax.axis_index("dp")
    experts_all = block_map.shape[0]
    per_group = block_map.shape[1] // nj
    rows, width = gate_dense.shape
    blocks = width // BLK
    tok, feats = tokens.shape
    nc = blocks // ny
    group = tok * ny
    owned_map = lax.dynamic_slice_in_dim(block_map, dp_index * per_group, per_group, 1)
    picks = owned_map - dp_index * blocks
    takes = jnp.sum((picks[:, :, None] == jnp.arange(blocks)[None, None, :]).astype(jnp.float32), axis=1)
    named = (routes[:, :, None] == jnp.arange(experts_all)[None, None, :]).astype(jnp.float32)
    named = jnp.sum(named * route_gates[None, :, None], axis=1)
    weight = jnp.sum(named[:, :, None] * takes[None, :, :], axis=1)
    weight = weight.reshape(tok, ny, nc).transpose(1, 0, 2)
    weight = jnp.broadcast_to(weight[:, :, :, None], (ny, tok, nc, BLK)).reshape(ny, tok, nc * BLK)

    half, full = jnp.bfloat16, jnp.float32
    dma = pltpu.SemaphoreType.DMA
    vmem = pl.BlockSpec(memory_space=pltpu.VMEM)
    mixed, d_tokens, gate_grad, up_grad, down_grad = pl.pallas_call(
        functools.partial(kernel, nj, ny, nc),
        out_shape=(
            jax.ShapeDtypeStruct((tok, feats), half),
            jax.ShapeDtypeStruct((tok, feats), half),
            jax.ShapeDtypeStruct((rows, width), half),
            jax.ShapeDtypeStruct((rows, width), half),
            jax.ShapeDtypeStruct((rows, width), half),
        ),
        in_specs=[vmem] * 6,
        out_specs=(vmem,) * 5,
        scratch_shapes=[
            pltpu.VMEM((2 * tok, feats), half),
            pltpu.VMEM((ny, 2 * tok, feats), half),
            pltpu.VMEM((nj, 2, group, feats), half),
            pltpu.VMEM((ny, tok, nc * BLK), full),
            pltpu.VMEM((nc, ny * rows, 3 * BLK), half),
            pltpu.VMEM((nc, nj, group, 3 * BLK), half),
            pltpu.VMEM((nc, nj, group, 3 * BLK), half),
            pltpu.VMEM((nc, nj, group, 3 * BLK), half),
            pltpu.VMEM((nc, ny * rows, 3 * BLK), half),
            pltpu.VMEM((2, nj * group, feats), full),
            pltpu.VMEM((nj, 2, group, feats), half),
            pltpu.VMEM((nj, 2, group, feats), half),
            pltpu.VMEM((ny, 2 * tok, feats), half),
            pltpu.VMEM((ny, 2 * tok, feats), half),
            dma((ny,)), dma((ny,)), dma((ny,)), dma((ny,)),
            dma((nj,)), dma((nj,)),
            dma((nc, 3, ny)), dma((nc, 3, ny)),
            dma((nc, nj)), dma((nc, nj)), dma((nc, nj)), dma((nc, nj)),
            dma((nc, 3, ny)), dma((nc, 3, ny)),
            dma((nj,)), dma((nj,)), dma((ny,)), dma((ny,)),
        ],
        compiler_params=pltpu.CompilerParams(
            collective_id=0, has_side_effects=True, vmem_limit_bytes=40 * 1024 * 1024
        ),
    )(tokens, d_out, gate_dense, up_dense, down_dense.T, weight)
    return (
        mixed,
        d_tokens,
        gate_grad.astype(jnp.float32),
        up_grad.astype(jnp.float32),
        down_grad.astype(jnp.float32).T,
    )


def solution(mesh):
    in_specs = (
        P("expert", "dp"),
        P("expert", "dp"),
        P("expert", "dp"),
        P("expert", "dp"),
        P("dp", "expert"),
        P(),
        P("expert", None),
        P(),
    )
    out_specs = (
        P("expert", "dp"),
        P("expert", "dp"),
        P("expert", "dp"),
        P("expert", "dp"),
        P("dp", "expert"),
    )
    return jax.shard_map(shards, mesh=mesh, in_specs=in_specs, out_specs=out_specs, check_vma=False)
```

```python
import functools

import jax
import jax.numpy as jnp
from jax import lax
from jax.experimental import pallas as pl
from jax.experimental.pallas import tpu as pltpu
from jax.sharding import PartitionSpec as P

BLK = 128
MESH = pl.DeviceIdType.MESH
HALF, FULL = jnp.bfloat16, jnp.float32


def contract(left, right, left_dim, right_dim):
    return lax.dot_general(left, right, (((left_dim,), (right_dim,)), ((), ())), preferred_element_type=FULL)


def widen(rows, lanes):
    fill = jnp.zeros(rows.shape[:-1] + (lanes - rows.shape[-1],), rows.dtype)
    return jnp.concatenate([rows, fill], axis=-1).astype(HALF)


def kernel(
    nj, ny, nc, per,
    tok_ref, cot_ref, routes_ref, map_ref, gates_ref, gate_ref, up_ref, down_ref,
    mixed_ref, dtok_ref, gate_out, up_out, down_out,
    xs, xt, xb, dyb, xtr, dytr, wts, wbuf, wall, part, rs_buf, rs_recv, ag, grads, acc,
    op_send, op_core, op_buf, op_recv, t_send, t_recv,
    xt_ss, xt_rs, xb_ss, xb_rs, xc_ss, wt_ss, wt_rs, wl_s, w_ss, w_rs, r_ss, r_rs, a_ss, a_rs, g_ss, g_rs,
    oc_ss, oc_rs, o_ss, o_rs, t_ss, t_rs,
):
    nz, nx = nj, nj // 2
    hops_down, hops_up = nz // 2, nz - 1 - nz // 2
    j = lax.axis_index("dp")
    e = lax.axis_index("expert")
    x_me, core = j // 2, lax.rem(j, 2)
    z, y = e // ny, lax.rem(e, ny)
    rows = gate_ref.shape[0]
    quarter = gate_ref.shape[1] // ny
    feats, padded = tok_ref.shape[1], xs.shape[1]
    group = 8 * ny
    tokens_all = nj * group

    def at_y(k):
        return (j, z * ny + k)

    def at_z(k):
        return (j, lax.rem(z + k + nz, nz) * ny + y)

    def at_x(k):
        return (2 * k + core, e)

    def at_t(k):
        return (z, j * ny + k)

    other_core = (2 * x_me + 1 - core, e)

    def others(n, me, body):
        def step(i, _):
            body(lax.rem(me + i, n))
            return 0

        lax.fori_loop(1, n, step, 0)

    def crossing(body, own):
        def step(k, _):
            same = jnp.logical_and(z == j, k == y)

            @pl.when(jnp.logical_not(same))
            def _():
                body(k)

            if own is not None:
                @pl.when(same)
                def _():
                    own(k)

            return 0

        lax.fori_loop(0, ny, step, 0)

    def remote(src, dst, ss, rs, device):
        return pltpu.make_async_remote_copy(
            src_ref=src, dst_ref=dst, send_sem=ss, recv_sem=rs, device_id=device, device_id_type=MESH
        )

    barrier = pltpu.get_barrier_semaphore()

    def greet(device):
        pl.semaphore_signal(barrier, inc=1, device_id=device, device_id_type=MESH)

    others(ny, y, lambda k: greet(at_y(k)))
    greet(at_z(1))
    greet(at_z(-1))
    others(nx, x_me, lambda k: greet(at_x(k)))
    greet(other_core)
    count = (ny - 1) + 2 + (nx - 1) + 1

    @pl.when(z != j)
    def _():
        def step(k, _):
            greet(at_t(k))
            return 0

        lax.fori_loop(0, ny, step, 0)

    xs[...] = widen(jnp.concatenate([tok_ref[...].astype(FULL), cot_ref[...].astype(FULL)], axis=0), padded)

    @pl.when(z != j)
    def _():
        pl.semaphore_wait(barrier, count + ny)

    @pl.when(z == j)
    def _():
        pl.semaphore_wait(barrier, count)

    def x_copy(k):
        return remote(xs, xt.at[y], xt_ss.at[k], xt_rs.at[y], at_t(k))

    def x_wait(k):
        return remote(xs, xt.at[k], xt_ss.at[k], xt_rs.at[k], at_t(k))

    def x_own(k):
        xt[k] = xs[...]

    crossing(lambda k: x_copy(k).start(), x_own)

    def columns(k, c):
        return pl.ds(pl.multiple_of(k * quarter + c * BLK, BLK), BLK)

    def band(k):
        return pl.ds(pl.multiple_of(k * rows, 16), rows)

    def w_copies(k, c, slot):
        return [
            remote(ref.at[:, columns(k, c)], wall.at[c, band(slot), pl.ds(i * BLK, BLK)],
                   w_ss.at[c, i, k], w_rs.at[c, i, slot], at_y(k))
            for i, ref in enumerate((gate_ref, up_ref, down_ref))
        ]

    def w_local(c):
        return [
            pltpu.make_async_copy(ref.at[:, columns(y, c)], wall.at[c, band(y), pl.ds(i * BLK, BLK)], wl_s.at[c, i])
            for i, ref in enumerate((gate_ref, up_ref, down_ref))
        ]

    def start_all(copies):
        for copy in copies:
            copy.start()

    def wait_all(copies):
        for copy in copies:
            copy.wait()

    def recv_all(copies):
        for copy in copies:
            copy.wait_recv()

    def send_all(copies):
        for copy in copies:
            copy.wait_send()

    others(ny, y, lambda k: start_all(w_copies(k, 0, y)))

    crossing(lambda k: x_wait(k).wait_recv(), None)
    landed = xt[...].astype(FULL)[:, :, :feats]
    xb[j] = jnp.concatenate(
        [landed[:, :8].reshape(group, feats), landed[:, 8:].reshape(group, feats)], axis=1
    ).astype(HALF)

    def xb_copy(k, slot):
        return remote(xb.at[slot], xb.at[slot], xb_ss.at[k], xb_rs.at[slot], at_x(k))

    def xc_copy(k, side):
        slot = 2 * k + side
        return remote(xb.at[slot], xb.at[slot], xc_ss.at[k], xb_rs.at[slot], other_core)

    others(nx, x_me, lambda k: xb_copy(k, j).start())
    xc_copy(x_me, core).start()
    for c in range(1, nc):
        others(ny, y, lambda k: start_all(w_copies(k, c, y)))
    for c in range(nc):
        start_all(w_local(c))

    experts = map_ref.shape[1]
    names = lax.broadcasted_iota(jnp.int32, (8, experts), 1)
    named = jnp.zeros((8, experts), FULL)
    for k in range(routes_ref.shape[1]):
        named = named + jnp.where(routes_ref[:, k : k + 1] == names, gates_ref[k], 0.0)
    picks = [map_ref[pl.ds(j * per + q, 1), :] - j * (ny * nc) for q in range(per)]
    for k in range(ny):
        for c in range(nc):
            takes = sum((pick == k * nc + c).astype(FULL) for pick in picks)
            weight = jnp.sum(named * takes, axis=1, keepdims=True)
            wts[k, :, c * BLK : (c + 1) * BLK] = jnp.broadcast_to(weight, (8, BLK))

    def wt_copy(k):
        return remote(wts.at[k], wbuf.at[y], wt_ss.at[k], wt_rs.at[y], at_y(k))

    def wt_wait(k):
        return remote(wts.at[k], wbuf.at[k], wt_ss.at[k], wt_rs.at[k], at_y(k))

    others(ny, y, lambda k: wt_copy(k).start())
    wbuf[y] = wts[y]

    def forward(k):
        xb_copy(k, 2 * k + core).wait_recv()
        xc_copy(k, core).start()

    others(nx, x_me, forward)

    def from_core(k, _):
        xc_copy(k, 1 - core).wait_recv()
        return 0

    lax.fori_loop(0, nx, from_core, 0)
    dyb[...] = xb[:, :, feats:].reshape(tokens_all, feats)

    def x_all():
        return xb[:, :, :feats].reshape(tokens_all, feats)

    def lane(down, s):
        return s - 1 if down else hops_down + s - 1

    def rs_copy(c, down, s):
        i = lane(down, s)
        return remote(rs_buf.at[c, i], rs_recv.at[c, i], r_ss.at[c, i], r_rs.at[c, i], at_z(-1 if down else 1))

    def rs_send(c, down, s):
        t = lax.rem(z - (hops_down - s + 1) + nz, nz) if down else lax.rem(z + (hops_up - s + 1), nz)
        value = part[c, t]
        if s > 1:
            value = value + rs_recv[c, lane(down, s - 1)].astype(FULL)
        rs_buf[c, lane(down, s)] = value.astype(HALF)
        rs_copy(c, down, s).start()

    def ag_copy(c, down, s, arriving):
        i = lane(not down, s)
        shift = s if arriving else s - 1
        slot = lax.rem(z + shift, nz) if down else lax.rem(z - shift + nz, nz)
        return remote(ag.at[c, slot], ag.at[c, slot], a_ss.at[c, i], a_rs.at[c, i], at_z(-1 if down else 1))

    def g_copies(k, c, slot):
        return [
            remote(grads.at[c, band(k), pl.ds(i * BLK, BLK)], ref.at[:, columns(slot, c)],
                   g_ss.at[c, i, k], g_rs.at[c, i, slot], at_y(k))
            for i, ref in enumerate((gate_out, up_out, down_out))
        ]

    def first(c):
        wait_all(w_local(c))
        others(ny, y, lambda k: recv_all(w_copies(k, c, k)))
        part[c, :, :, 0 : 2 * BLK] = contract(x_all(), wall[c, :, 0 : 2 * BLK], 1, 0).reshape(nz, group, 2 * BLK)
        part[c, :, :, 2 * BLK : 3 * BLK] = contract(dyb[...], wall[c, :, 2 * BLK : 3 * BLK], 1, 0).reshape(nz, group, BLK)
        rs_send(c, True, 1)
        if hops_up:
            rs_send(c, False, 1)

    def middle(c):
        if c == 0:
            others(ny, y, lambda k: wt_wait(k).wait_recv())
        total = part[c, z] + rs_recv[c, lane(True, hops_down)].astype(FULL)
        if hops_up:
            total = total + rs_recv[c, lane(False, hops_up)].astype(FULL)
        gate_pre, up_pre, hidden_grad = total[:, :BLK], total[:, BLK : 2 * BLK], total[:, 2 * BLK :]
        weight = wbuf[:, :, c * BLK : (c + 1) * BLK].reshape(group, BLK)
        sigma = jax.nn.sigmoid(gate_pre)
        silu = gate_pre * sigma
        scaled = weight * hidden_grad
        ag[c, z, :, 0:BLK] = (scaled * up_pre * sigma * (1.0 + gate_pre * (1.0 - sigma))).astype(HALF)
        ag[c, z, :, BLK : 2 * BLK] = (scaled * silu).astype(HALF)
        ag[c, z, :, 2 * BLK : 3 * BLK] = (weight * silu * up_pre).astype(HALF)
        ag_copy(c, False, 1, False).start()
        if hops_up:
            ag_copy(c, True, 1, False).start()

    def last(c):
        pair = ag[c, :, :, 0 : 2 * BLK].reshape(tokens_all, 2 * BLK)
        hidden = ag[c, :, :, 2 * BLK : 3 * BLK].reshape(tokens_all, BLK)

        def block_grads():
            grads[c, :, 0 : 2 * BLK] = contract(xtr[...], pair, 1, 0).astype(HALF)
            grads[c, :, 2 * BLK : 3 * BLK] = contract(dytr[...], hidden, 1, 0).astype(HALF)
            others(ny, y, lambda k: start_all(g_copies(k, c, y)))

        if c < nc - 1:
            block_grads()
        out_part = contract(hidden, wall[c, :, 2 * BLK : 3 * BLK], 1, 1)
        in_part = contract(pair, wall[c, :, 0 : 2 * BLK], 1, 1)
        if c > 0:
            out_part = out_part + acc[0]
            in_part = in_part + acc[1]
        if c < nc - 1:
            acc[0], acc[1] = out_part, in_part
        else:
            parts = jnp.concatenate([out_part, in_part], axis=1).reshape(nx, 2, group, 2 * feats)
            op_send[...] = parts.astype(HALF)
            others(nx, x_me, lambda k: oc_copy(k).start())
            oc_copy(x_me).start()
            block_grads()

    def oc_copy(k):
        return remote(op_send.at[k, 1 - core], op_core.at[k], oc_ss.at[k], oc_rs.at[k], other_core)

    def op_copy(k, slot):
        return remote(op_buf.at[k], op_recv.at[slot], o_ss.at[k], o_rs.at[slot], at_x(k))

    def stage(c, s):
        if s == 0:
            first(c)
        elif s <= hops_down:
            rs_copy(c, True, s).wait_recv()
            if s < hops_down:
                rs_send(c, True, s + 1)
            if s <= hops_up:
                rs_copy(c, False, s).wait_recv()
                if s < hops_up:
                    rs_send(c, False, s + 1)
            if s == hops_down:
                middle(c)
        else:
            s = s - hops_down
            ag_copy(c, False, s, True).wait_recv()
            if s < hops_down:
                ag_copy(c, False, s + 1, False).start()
            if s <= hops_up:
                ag_copy(c, True, s, True).wait_recv()
                if s < hops_up:
                    ag_copy(c, True, s + 1, False).start()
            if s == hops_down:
                last(c)

    stages = 2 * hops_down + 1
    for slot in range(stages + nc - 1):
        for c in reversed(range(nc)):
            if 0 <= slot - c < stages:
                stage(c, slot - c)
        if slot == nc - 1:
            xtr[...] = x_all().T
            dytr[...] = dyb[...].T

    def pass_on(k):
        oc_copy(k).wait_recv()
        op_buf[k] = (op_send[k, core].astype(FULL) + op_core[k].astype(FULL)).astype(HALF)
        op_copy(k, x_me).start()

    others(nx, x_me, pass_on)
    oc_copy(x_me).wait_recv()
    for c in range(nc):
        for i, ref in enumerate((gate_out, up_out, down_out)):
            ref[:, columns(y, c)] = grads[c, band(y), i * BLK : (i + 1) * BLK]
    op_recv[x_me] = op_core[x_me]
    others(nx, x_me, lambda k: op_copy(k, k).wait_recv())
    summed = jnp.sum(op_recv[...].astype(FULL), axis=0) + op_send[x_me, core].astype(FULL)
    t_send[...] = widen(
        jnp.concatenate(
            [summed[:, :feats].reshape(ny, 8, feats), summed[:, feats:].reshape(ny, 8, feats)], axis=1
        ),
        padded,
    )

    def t_copy(k):
        return remote(t_send.at[k], t_recv.at[y], t_ss.at[k], t_rs.at[y], at_t(k))

    def t_wait(k):
        return remote(t_send.at[k], t_recv.at[k], t_ss.at[k], t_rs.at[k], at_t(k))

    def t_own(k):
        t_recv[k] = t_send[k]

    crossing(lambda k: t_copy(k).start(), t_own)

    for c in range(nc):
        others(ny, y, lambda k: recv_all(g_copies(k, c, k)))
    crossing(lambda k: x_copy(k).wait_send(), None)
    others(ny, y, lambda k: wt_copy(k).wait_send())
    others(nx, x_me, lambda k: xb_copy(k, j).wait_send())
    for k in range(nx):
        xc_copy(k, core).wait_send()
        oc_copy(k).wait_send()
    others(nx, x_me, lambda k: op_copy(k, x_me).wait_send())
    for c in range(nc):
        others(ny, y, lambda k: send_all(w_copies(k, c, y)))
        for down, hops in ((True, hops_down), (False, hops_up)):
            for s in range(1, hops + 1):
                rs_copy(c, down, s).wait_send()
                ag_copy(c, not down, s, False).wait_send()
        others(ny, y, lambda k: send_all(g_copies(k, c, y)))

    crossing(lambda k: t_wait(k).wait_recv(), None)
    final = jnp.sum(t_recv[...].astype(FULL), axis=0)
    mixed_ref[...] = final[:8, :feats].astype(HALF)
    dtok_ref[...] = final[8:, :feats].astype(HALF)
    crossing(lambda k: t_copy(k).wait_send(), None)


def finish(mixed_ref, dtok_ref, gate_ref, up_ref, down_ref, mixed_out, dtok_out, gate_out, up_out, down_out):
    mixed_out[...] = mixed_ref[...]
    dtok_out[...] = dtok_ref[...]
    for source, target in ((gate_ref, gate_out), (up_ref, up_out), (down_ref, down_out)):
        target[...] = source[...].astype(FULL)


def shards(tokens, d_out, gate_dense, up_dense, down_dense, block_map, routes, route_gates):
    nj = lax.axis_size("dp")
    ny = lax.axis_size("expert") // nj
    nx = nj // 2
    per = block_map.shape[1] // nj
    rows, width = gate_dense.shape
    tok, feats = tokens.shape
    nc = width // BLK // ny
    group = tok * ny
    padded = -(-feats // BLK) * BLK
    hops = nj - 1
    dma = pltpu.SemaphoreType.DMA
    vmem = pl.BlockSpec(memory_space=pltpu.VMEM)
    smem = pl.BlockSpec(memory_space=pltpu.SMEM)
    hbm = pl.BlockSpec(memory_space=pltpu.HBM)
    outs = (
        jax.ShapeDtypeStruct((tok, feats), HALF),
        jax.ShapeDtypeStruct((tok, feats), HALF),
    ) + (jax.ShapeDtypeStruct((rows, width), HALF),) * 3
    results = pl.pallas_call(
        functools.partial(kernel, nj, ny, nc, per),
        out_shape=outs,
        in_specs=[vmem] * 4 + [smem] + [hbm] * 3,
        out_specs=(vmem,) * 5,
        scratch_shapes=[
            pltpu.VMEM((2 * tok, padded), HALF),
            pltpu.VMEM((ny, 2 * tok, padded), HALF),
            pltpu.VMEM((nj, group, 2 * feats), HALF),
            pltpu.VMEM((nj * group, feats), HALF),
            pltpu.VMEM((feats, nj * group), HALF),
            pltpu.VMEM((feats, nj * group), HALF),
            pltpu.VMEM((ny, tok, nc * BLK), FULL),
            pltpu.VMEM((ny, tok, nc * BLK), FULL),
            pltpu.VMEM((nc, ny * rows, 3 * BLK), HALF),
            pltpu.VMEM((nc, nj, group, 3 * BLK), FULL),
            pltpu.VMEM((nc, hops, group, 3 * BLK), HALF),
            pltpu.VMEM((nc, hops, group, 3 * BLK), HALF),
            pltpu.VMEM((nc, nj, group, 3 * BLK), HALF),
            pltpu.VMEM((nc, ny * rows, 3 * BLK), HALF),
            pltpu.VMEM((2, nj * group, feats), FULL),
            pltpu.VMEM((nx, 2, group, 2 * feats), HALF),
            pltpu.VMEM((nx, group, 2 * feats), HALF),
            pltpu.VMEM((nx, group, 2 * feats), HALF),
            pltpu.VMEM((nx, group, 2 * feats), HALF),
            pltpu.VMEM((ny, 2 * tok, padded), HALF),
            pltpu.VMEM((ny, 2 * tok, padded), HALF),
            dma((ny,)), dma((ny,)), dma((nx,)), dma((nj,)), dma((nx,)),
            dma((ny,)), dma((ny,)), dma((nc, 3)),
            dma((nc, 3, ny)), dma((nc, 3, ny)),
            dma((nc, hops)), dma((nc, hops)), dma((nc, hops)), dma((nc, hops)),
            dma((nc, 3, ny)), dma((nc, 3, ny)),
            dma((nx,)), dma((nx,)), dma((nx,)), dma((nx,)), dma((ny,)), dma((ny,)),
        ],
        compiler_params=pltpu.CompilerParams(
            collective_id=0, has_side_effects=True, vmem_limit_bytes=40 * 1024 * 1024
        ),
    )(tokens, d_out, routes, block_map.T, route_gates, gate_dense, up_dense, down_dense.T)
    mixed, d_tokens, gate_grad, up_grad, down_grad = pl.pallas_call(
        finish,
        out_shape=outs[:2] + (jax.ShapeDtypeStruct((rows, width), FULL),) * 3,
        in_specs=[vmem] * 5,
        out_specs=(vmem,) * 5,
        compiler_params=pltpu.CompilerParams(vmem_limit_bytes=16 * 1024 * 1024),
    )(*results)
    return mixed, d_tokens, gate_grad, up_grad, down_grad.T


def solution(mesh):
    in_specs = (
        P("expert", "dp"),
        P("expert", "dp"),
        P("expert", "dp"),
        P("expert", "dp"),
        P("dp", "expert"),
        P(),
        P("expert", None),
        P(),
    )
    out_specs = (
        P("expert", "dp"),
        P("expert", "dp"),
        P("expert", "dp"),
        P("expert", "dp"),
        P("dp", "expert"),
    )
    return jax.shard_map(shards, mesh=mesh, in_specs=in_specs, out_specs=out_specs, check_vma=False)
```

```python
import functools

import jax
import jax.numpy as jnp
from jax import lax
from jax.experimental import pallas as pl
from jax.experimental.pallas import tpu as pltpu
from jax.sharding import PartitionSpec as P

BLK = 128
MESH = pl.DeviceIdType.MESH
LIMIT = 60 * 1024 * 1024
HALF, FULL = jnp.bfloat16, jnp.float32


def contract(left, right, left_dim, right_dim):
    return lax.dot_general(left, right, (((left_dim,), (right_dim,)), ((), ())), preferred_element_type=FULL)


def widen(rows, lanes):
    fill = jnp.zeros(rows.shape[:-1] + (lanes - rows.shape[-1],), rows.dtype)
    return jnp.concatenate([rows, fill], axis=-1).astype(HALF)


def kernel(
    nj, ny, nc, per,
    tok_hbm, cot_hbm, routes_hbm, map_hbm, gates_hbm, gate_ref, up_ref, down_ref,
    mixed_ref, dtok_ref, gate_out, up_out, down_out,
    xs, xt, xb, dyb, xtr, dytr, wts, wbuf, wall, part, rs_buf, rs_recv, ag, grads, acc,
    op_send, op_core, op_buf, op_recv, t_send, t_recv,
    tok_ref, cot_ref, routes_ref, map_ref, gates_ref, in_s, own_s,
    xt_ss, xt_rs, xb_ss, xb_rs, xc_ss, wt_ss, wt_rs, wl_s, w_ss, w_rs, r_ss, r_rs, a_ss, a_rs, g_ss, g_rs,
    oc_ss, oc_rs, o_ss, o_rs, t_ss, t_rs,
):
    nz, nx = nj, nj // 2
    hops_down, hops_up = nz // 2, nz - 1 - nz // 2
    j = lax.axis_index("dp")
    e = lax.axis_index("expert")
    x_me, core = j // 2, lax.rem(j, 2)
    z, y = e // ny, lax.rem(e, ny)
    rows = gate_ref.shape[0]
    quarter = gate_ref.shape[1] // ny
    feats, padded = tok_hbm.shape[1], xs.shape[1]
    group = 8 * ny
    tokens_all = nj * group

    def at_y(k):
        return (j, z * ny + k)

    def at_z(k):
        return (j, lax.rem(z + k + nz, nz) * ny + y)

    def at_x(k):
        return (2 * k + core, e)

    def at_t(k):
        return (z, j * ny + k)

    other_core = (2 * x_me + 1 - core, e)

    def others(n, me, body):
        def step(i, _):
            body(lax.rem(me + i, n))
            return 0

        lax.fori_loop(1, n, step, 0)

    def crossing(body, own):
        def step(k, _):
            same = jnp.logical_and(z == j, k == y)

            @pl.when(jnp.logical_not(same))
            def _():
                body(k)

            if own is not None:
                @pl.when(same)
                def _():
                    own(k)

            return 0

        lax.fori_loop(0, ny, step, 0)

    def remote(src, dst, ss, rs, device):
        return pltpu.make_async_remote_copy(
            src_ref=src, dst_ref=dst, send_sem=ss, recv_sem=rs, device_id=device, device_id_type=MESH
        )

    small = [
        pltpu.make_async_copy(source, target, in_s.at[i])
        for i, (source, target) in enumerate(
            ((tok_hbm, tok_ref), (cot_hbm, cot_ref), (routes_hbm, routes_ref), (map_hbm, map_ref), (gates_hbm, gates_ref))
        )
    ]
    for copy in small:
        copy.start()

    barrier = pltpu.get_barrier_semaphore()

    def greet(device):
        pl.semaphore_signal(barrier, inc=1, device_id=device, device_id_type=MESH)

    others(ny, y, lambda k: greet(at_y(k)))
    greet(at_z(1))
    greet(at_z(-1))
    others(nx, x_me, lambda k: greet(at_x(k)))
    greet(other_core)
    count = (ny - 1) + 2 + (nx - 1) + 1

    @pl.when(z != j)
    def _():
        def step(k, _):
            greet(at_t(k))
            return 0

        lax.fori_loop(0, ny, step, 0)

    for copy in small:
        copy.wait()
    xs[...] = widen(jnp.concatenate([tok_ref[...].astype(FULL), cot_ref[...].astype(FULL)], axis=0), padded)

    @pl.when(z != j)
    def _():
        pl.semaphore_wait(barrier, count + ny)

    @pl.when(z == j)
    def _():
        pl.semaphore_wait(barrier, count)

    def x_copy(k):
        return remote(xs, xt.at[y], xt_ss.at[k], xt_rs.at[y], at_t(k))

    def x_wait(k):
        return remote(xs, xt.at[k], xt_ss.at[k], xt_rs.at[k], at_t(k))

    def x_own(k):
        xt[k] = xs[...]

    crossing(lambda k: x_copy(k).start(), x_own)

    def columns(k, c):
        return pl.ds(pl.multiple_of(k * quarter + c * BLK, BLK), BLK)

    def band(k):
        return pl.ds(pl.multiple_of(k * rows, 16), rows)

    def w_copies(k, c, slot):
        return [
            remote(ref.at[:, columns(k, c)], wall.at[c, band(slot), pl.ds(i * BLK, BLK)],
                   w_ss.at[c, i, k], w_rs.at[c, i, slot], at_y(k))
            for i, ref in enumerate((gate_ref, up_ref, down_ref))
        ]

    def w_local(c):
        return [
            pltpu.make_async_copy(ref.at[:, columns(y, c)], wall.at[c, band(y), pl.ds(i * BLK, BLK)], wl_s.at[c, i])
            for i, ref in enumerate((gate_ref, up_ref, down_ref))
        ]

    def start_all(copies):
        for copy in copies:
            copy.start()

    def wait_all(copies):
        for copy in copies:
            copy.wait()

    def recv_all(copies):
        for copy in copies:
            copy.wait_recv()

    def send_all(copies):
        for copy in copies:
            copy.wait_send()

    experts = map_ref.shape[1]
    names = lax.broadcasted_iota(jnp.int32, (8, experts), 1)
    named = jnp.zeros((8, experts), FULL)
    for k in range(routes_ref.shape[1]):
        named = named + jnp.where(routes_ref[:, k : k + 1] == names, gates_ref[:, k : k + 1], 0.0)
    picks = [map_ref[pl.ds(j * per + q, 1), :] - j * (ny * nc) for q in range(per)]
    for k in range(ny):
        for c in range(nc):
            takes = sum((pick == k * nc + c).astype(FULL) for pick in picks)
            weight = jnp.sum(named * takes, axis=1, keepdims=True)
            wts[k, :, c * BLK : (c + 1) * BLK] = jnp.broadcast_to(weight, (8, BLK))

    def wt_copy(k):
        return remote(wts.at[k], wbuf.at[y], wt_ss.at[k], wt_rs.at[y], at_y(k))

    def wt_wait(k):
        return remote(wts.at[k], wbuf.at[k], wt_ss.at[k], wt_rs.at[k], at_y(k))

    others(ny, y, lambda k: wt_copy(k).start())
    wbuf[y] = wts[y]

    others(ny, y, lambda k: start_all(w_copies(k, 0, y)))

    crossing(lambda k: x_wait(k).wait_recv(), None)
    landed = xt[...].astype(FULL)[:, :, :feats]
    xb[j] = jnp.concatenate(
        [landed[:, :8].reshape(group, feats), landed[:, 8:].reshape(group, feats)], axis=1
    ).astype(HALF)

    def xb_copy(k, slot):
        return remote(xb.at[slot], xb.at[slot], xb_ss.at[k], xb_rs.at[slot], at_x(k))

    def xc_copy(k, side):
        slot = 2 * k + side
        return remote(xb.at[slot], xb.at[slot], xc_ss.at[k], xb_rs.at[slot], other_core)

    others(nx, x_me, lambda k: xb_copy(k, j).start())
    xc_copy(x_me, core).start()
    for c in range(1, nc):
        others(ny, y, lambda k: start_all(w_copies(k, c, y)))
    for c in range(nc):
        start_all(w_local(c))

    def forward(k):
        xb_copy(k, 2 * k + core).wait_recv()
        xc_copy(k, core).start()

    for k in sorted(range(1, nx), key=lambda k: min(k, nx - k)):
        forward(lax.rem(x_me + k, nx))

    def from_core(k, _):
        xc_copy(k, 1 - core).wait_recv()
        return 0

    lax.fori_loop(0, nx, from_core, 0)
    dyb[...] = xb[:, :, feats:].reshape(tokens_all, feats)

    def x_all():
        return xb[:, :, :feats].reshape(tokens_all, feats)

    def lane(down, s):
        return s - 1 if down else hops_down + s - 1

    def rs_copy(c, down, s):
        i = lane(down, s)
        return remote(rs_buf.at[c, i], rs_recv.at[c, i], r_ss.at[c, i], r_rs.at[c, i], at_z(-1 if down else 1))

    def rs_send(c, down, s):
        t = lax.rem(z - (hops_down - s + 1) + nz, nz) if down else lax.rem(z + (hops_up - s + 1), nz)
        value = part[c, t]
        if s > 1:
            value = value + rs_recv[c, lane(down, s - 1)].astype(FULL)
        rs_buf[c, lane(down, s)] = value.astype(HALF)
        rs_copy(c, down, s).start()

    def ag_copy(c, down, s, arriving):
        i = lane(not down, s)
        shift = s if arriving else s - 1
        slot = lax.rem(z + shift, nz) if down else lax.rem(z - shift + nz, nz)
        return remote(ag.at[c, slot], ag.at[c, slot], a_ss.at[c, i], a_rs.at[c, i], at_z(-1 if down else 1))

    def g_copies(k, c, slot):
        return [
            remote(grads.at[c, band(k), pl.ds(i * BLK, BLK)], ref.at[:, columns(slot, c)],
                   g_ss.at[c, i, k], g_rs.at[c, i, slot], at_y(k))
            for i, ref in enumerate((gate_out, up_out, down_out))
        ]

    def g_local(c):
        return [
            pltpu.make_async_copy(grads.at[c, band(y), pl.ds(i * BLK, BLK)], ref.at[:, columns(y, c)], own_s.at[c, i])
            for i, ref in enumerate((gate_out, up_out, down_out))
        ]

    def first(c):
        wait_all(w_local(c))
        others(ny, y, lambda k: recv_all(w_copies(k, c, k)))
        part[c, :, :, 0 : 2 * BLK] = contract(x_all(), wall[c, :, 0 : 2 * BLK], 1, 0).reshape(nz, group, 2 * BLK)
        part[c, :, :, 2 * BLK : 3 * BLK] = contract(dyb[...], wall[c, :, 2 * BLK : 3 * BLK], 1, 0).reshape(nz, group, BLK)
        rs_send(c, True, 1)
        if hops_up:
            rs_send(c, False, 1)

    def middle(c):
        if c == 0:
            others(ny, y, lambda k: wt_wait(k).wait_recv())
        total = part[c, z] + rs_recv[c, lane(True, hops_down)].astype(FULL)
        if hops_up:
            total = total + rs_recv[c, lane(False, hops_up)].astype(FULL)
        gate_pre, up_pre, hidden_grad = total[:, :BLK], total[:, BLK : 2 * BLK], total[:, 2 * BLK :]
        weight = wbuf[:, :, c * BLK : (c + 1) * BLK].reshape(group, BLK)
        sigma = jax.nn.sigmoid(gate_pre)
        silu = gate_pre * sigma
        scaled = weight * hidden_grad
        ag[c, z, :, 0:BLK] = (scaled * up_pre * sigma * (1.0 + gate_pre * (1.0 - sigma))).astype(HALF)
        ag[c, z, :, BLK : 2 * BLK] = (scaled * silu).astype(HALF)
        ag[c, z, :, 2 * BLK : 3 * BLK] = (weight * silu * up_pre).astype(HALF)
        ag_copy(c, False, 1, False).start()
        if hops_up:
            ag_copy(c, True, 1, False).start()

    def last(c):
        pair = ag[c, :, :, 0 : 2 * BLK].reshape(tokens_all, 2 * BLK)
        hidden = ag[c, :, :, 2 * BLK : 3 * BLK].reshape(tokens_all, BLK)

        def block_grads():
            grads[c, :, 0 : 2 * BLK] = contract(xtr[...], pair, 1, 0).astype(HALF)
            grads[c, :, 2 * BLK : 3 * BLK] = contract(dytr[...], hidden, 1, 0).astype(HALF)
            others(ny, y, lambda k: start_all(g_copies(k, c, y)))
            start_all(g_local(c))

        if c < nc - 1:
            block_grads()
        out_part = contract(hidden, wall[c, :, 2 * BLK : 3 * BLK], 1, 1)
        in_part = contract(pair, wall[c, :, 0 : 2 * BLK], 1, 1)
        if c > 0:
            out_part = out_part + acc[0]
            in_part = in_part + acc[1]
        if c < nc - 1:
            acc[0], acc[1] = out_part, in_part
        else:
            parts = jnp.concatenate([out_part, in_part], axis=1).reshape(nx, 2, group, 2 * feats)
            op_send[...] = parts.astype(HALF)
            for k in sorted(range(1, nx), key=lambda k: -min(k, nx - k)):
                oc_copy(lax.rem(x_me + k, nx)).start()
            oc_copy(x_me).start()
            block_grads()

    def oc_copy(k):
        return remote(op_send.at[k, 1 - core], op_core.at[k], oc_ss.at[k], oc_rs.at[k], other_core)

    def op_copy(k, slot):
        return remote(op_buf.at[k], op_recv.at[slot], o_ss.at[k], o_rs.at[slot], at_x(k))

    def stage(c, s):
        if s == 0:
            first(c)
        elif s <= hops_down:
            rs_copy(c, True, s).wait_recv()
            if s < hops_down:
                rs_send(c, True, s + 1)
            if s <= hops_up:
                rs_copy(c, False, s).wait_recv()
                if s < hops_up:
                    rs_send(c, False, s + 1)
            if s == hops_down:
                middle(c)
        else:
            s = s - hops_down
            ag_copy(c, False, s, True).wait_recv()
            if s < hops_down:
                ag_copy(c, False, s + 1, False).start()
            if s <= hops_up:
                ag_copy(c, True, s, True).wait_recv()
                if s < hops_up:
                    ag_copy(c, True, s + 1, False).start()
            if s == hops_down:
                last(c)

    stages = 2 * hops_down + 1
    for slot in range(stages + nc - 1):
        for c in reversed(range(nc)):
            if 0 <= slot - c < stages:
                stage(c, slot - c)
        if slot == nc - 1:
            xtr[...] = x_all().T
            dytr[...] = dyb[...].T

    def pass_on(k):
        oc_copy(k).wait_recv()
        op_buf[k] = (op_send[k, core].astype(FULL) + op_core[k].astype(FULL)).astype(HALF)
        op_copy(k, x_me).start()

    for k in sorted(range(1, nx), key=lambda k: -min(k, nx - k)):
        pass_on(lax.rem(x_me + k, nx))
    oc_copy(x_me).wait_recv()
    op_recv[x_me] = op_core[x_me]
    others(nx, x_me, lambda k: op_copy(k, k).wait_recv())
    summed = jnp.sum(op_recv[...].astype(FULL), axis=0) + op_send[x_me, core].astype(FULL)
    t_send[...] = widen(
        jnp.concatenate(
            [summed[:, :feats].reshape(ny, 8, feats), summed[:, feats:].reshape(ny, 8, feats)], axis=1
        ),
        padded,
    )

    def t_copy(k):
        return remote(t_send.at[k], t_recv.at[y], t_ss.at[k], t_rs.at[y], at_t(k))

    def t_wait(k):
        return remote(t_send.at[k], t_recv.at[k], t_ss.at[k], t_rs.at[k], at_t(k))

    def t_own(k):
        t_recv[k] = t_send[k]

    crossing(lambda k: t_copy(k).start(), t_own)

    for c in range(nc):
        others(ny, y, lambda k: recv_all(g_copies(k, c, k)))
    crossing(lambda k: x_copy(k).wait_send(), None)
    others(ny, y, lambda k: wt_copy(k).wait_send())
    others(nx, x_me, lambda k: xb_copy(k, j).wait_send())
    for k in range(nx):
        xc_copy(k, core).wait_send()
        oc_copy(k).wait_send()
    others(nx, x_me, lambda k: op_copy(k, x_me).wait_send())
    for c in range(nc):
        others(ny, y, lambda k: send_all(w_copies(k, c, y)))
        for down, hops in ((True, hops_down), (False, hops_up)):
            for s in range(1, hops + 1):
                rs_copy(c, down, s).wait_send()
                ag_copy(c, not down, s, False).wait_send()
        others(ny, y, lambda k: send_all(g_copies(k, c, y)))
        wait_all(g_local(c))

    crossing(lambda k: t_wait(k).wait_recv(), None)
    final = jnp.sum(t_recv[...].astype(FULL), axis=0)
    mixed_ref[...] = final[:8, :feats].astype(HALF)
    dtok_ref[...] = final[8:, :feats].astype(HALF)
    crossing(lambda k: t_copy(k).wait_send(), None)


def finish(mixed_ref, dtok_ref, gate_ref, up_ref, down_ref, mixed_out, dtok_out, gate_out, up_out, down_out):
    mixed_out[...] = mixed_ref[...]
    dtok_out[...] = dtok_ref[...]
    for source, target in ((gate_ref, gate_out), (up_ref, up_out), (down_ref, down_out)):
        target[...] = source[...].astype(FULL)


def shards(tokens, d_out, gate_dense, up_dense, down_dense, block_map, routes, route_gates):
    nj = lax.axis_size("dp")
    ny = lax.axis_size("expert") // nj
    nx = nj // 2
    per = block_map.shape[1] // nj
    rows, width = gate_dense.shape
    tok, feats = tokens.shape
    nc = width // BLK // ny
    group = tok * ny
    padded = -(-feats // BLK) * BLK
    hops = nj - 1
    dma = pltpu.SemaphoreType.DMA
    vmem = pl.BlockSpec(memory_space=pltpu.VMEM)
    hbm = pl.BlockSpec(memory_space=pltpu.HBM)
    outs = (
        jax.ShapeDtypeStruct((tok, feats), HALF),
        jax.ShapeDtypeStruct((tok, feats), HALF),
    ) + (jax.ShapeDtypeStruct((rows, width), HALF),) * 3
    results = pl.pallas_call(
        functools.partial(kernel, nj, ny, nc, per),
        out_shape=outs,
        in_specs=[hbm] * 8,
        out_specs=(vmem,) * 2 + (hbm,) * 3,
        scratch_shapes=[
            pltpu.VMEM((2 * tok, padded), HALF),
            pltpu.VMEM((ny, 2 * tok, padded), HALF),
            pltpu.VMEM((nj, group, 2 * feats), HALF),
            pltpu.VMEM((nj * group, feats), HALF),
            pltpu.VMEM((feats, nj * group), HALF),
            pltpu.VMEM((feats, nj * group), HALF),
            pltpu.VMEM((ny, tok, nc * BLK), FULL),
            pltpu.VMEM((ny, tok, nc * BLK), FULL),
            pltpu.VMEM((nc, ny * rows, 3 * BLK), HALF),
            pltpu.VMEM((nc, nj, group, 3 * BLK), FULL),
            pltpu.VMEM((nc, hops, group, 3 * BLK), HALF),
            pltpu.VMEM((nc, hops, group, 3 * BLK), HALF),
            pltpu.VMEM((nc, nj, group, 3 * BLK), HALF),
            pltpu.VMEM((nc, ny * rows, 3 * BLK), HALF),
            pltpu.VMEM((2, nj * group, feats), FULL),
            pltpu.VMEM((nx, 2, group, 2 * feats), HALF),
            pltpu.VMEM((nx, group, 2 * feats), HALF),
            pltpu.VMEM((nx, group, 2 * feats), HALF),
            pltpu.VMEM((nx, group, 2 * feats), HALF),
            pltpu.VMEM((ny, 2 * tok, padded), HALF),
            pltpu.VMEM((ny, 2 * tok, padded), HALF),
            pltpu.VMEM((tok, feats), HALF),
            pltpu.VMEM((tok, feats), HALF),
            pltpu.VMEM(routes.shape, jnp.int32),
            pltpu.VMEM(block_map.shape[::-1], jnp.int32),
            pltpu.VMEM((1, routes.shape[1]), FULL),
            dma((5,)), dma((nc, 3)),
            dma((ny,)), dma((ny,)), dma((nx,)), dma((nj,)), dma((nx,)),
            dma((ny,)), dma((ny,)), dma((nc, 3)),
            dma((nc, 3, ny)), dma((nc, 3, ny)),
            dma((nc, hops)), dma((nc, hops)), dma((nc, hops)), dma((nc, hops)),
            dma((nc, 3, ny)), dma((nc, 3, ny)),
            dma((nx,)), dma((nx,)), dma((nx,)), dma((nx,)), dma((ny,)), dma((ny,)),
        ],
        compiler_params=pltpu.CompilerParams(
            collective_id=0, has_side_effects=True, vmem_limit_bytes=LIMIT
        ),
    )(tokens, d_out, routes, block_map.T, route_gates.reshape(1, -1), gate_dense, up_dense, down_dense.T)
    steps = 3
    small_spec = pl.BlockSpec((tok, feats), lambda i: (0, 0))
    wide = pl.BlockSpec((rows, width // steps), lambda i: (0, i))
    mixed, d_tokens, gate_grad, up_grad, down_grad = pl.pallas_call(
        finish,
        grid=(steps,),
        out_shape=outs[:2] + (jax.ShapeDtypeStruct((rows, width), FULL),) * 3,
        in_specs=[small_spec] * 2 + [wide] * 3,
        out_specs=(small_spec,) * 2 + (wide,) * 3,
        compiler_params=pltpu.CompilerParams(vmem_limit_bytes=LIMIT),
    )(*results)
    return mixed, d_tokens, gate_grad, up_grad, down_grad.T


def solution(mesh):
    in_specs = (
        P("expert", "dp"),
        P("expert", "dp"),
        P("expert", "dp"),
        P("expert", "dp"),
        P("dp", "expert"),
        P(),
        P("expert", None),
        P(),
    )
    out_specs = (
        P("expert", "dp"),
        P("expert", "dp"),
        P("expert", "dp"),
        P("expert", "dp"),
        P("dp", "expert"),
    )
    return jax.shard_map(shards, mesh=mesh, in_specs=in_specs, out_specs=out_specs, check_vma=False)
```

```python
import functools

import jax
import jax.numpy as jnp
from jax import lax
from jax.experimental import pallas as pl
from jax.experimental.pallas import tpu as pltpu
from jax.sharding import PartitionSpec as P

BLK = 128
MESH = pl.DeviceIdType.MESH
LIMIT = 60 * 1024 * 1024
HALF, FULL = jnp.bfloat16, jnp.float32


def contract(left, right, left_dim, right_dim):
    return lax.dot_general(left, right, (((left_dim,), (right_dim,)), ((), ())), preferred_element_type=FULL)


def widen(rows, lanes):
    fill = jnp.zeros(rows.shape[:-1] + (lanes - rows.shape[-1],), rows.dtype)
    return jnp.concatenate([rows, fill], axis=-1).astype(HALF)


def kernel(
    nj, ny, nc, per,
    tok_hbm, cot_hbm, routes_hbm, map_hbm, gates_hbm, gate_ref, up_ref, down_ref,
    mixed_ref, dtok_ref, gate_out, up_out, down_out,
    xs, xt, xb, dyb, xtr, dytr, wts, wbuf, wall, part, rs_buf, rs_recv, ag, grads, acc,
    op_send, op_core, op_buf, op_recv, t_send, t_recv,
    tok_ref, cot_ref, routes_ref, map_ref, gates_ref, in_s, own_s,
    xt_ss, xt_rs, xb_ss, xb_rs, xc_ss, wt_ss, wt_rs, wl_s, w_ss, w_rs, r_ss, r_rs, a_ss, a_rs, g_ss, g_rs,
    oc_ss, oc_rs, o_ss, o_rs, t_ss, t_rs,
):
    nz, nx = nj, nj // 2
    j = lax.axis_index("dp")
    e = lax.axis_index("expert")
    x_me, core = j // 2, lax.rem(j, 2)
    z, y = e // ny, lax.rem(e, ny)
    rows = gate_ref.shape[0]
    quarter = gate_ref.shape[1] // ny
    feats, padded = tok_hbm.shape[1], xs.shape[1]
    group = 8 * ny
    tokens_all = nj * group

    def at_y(k):
        return (j, z * ny + k)

    def at_z(k):
        return (j, lax.rem(z + k + nz, nz) * ny + y)

    def at_x(k):
        return (2 * k + core, e)

    def at_t(k):
        return (z, j * ny + k)

    other_core = (2 * x_me + 1 - core, e)

    def others(n, me, body):
        def step(i, _):
            body(lax.rem(me + i, n))
            return 0

        lax.fori_loop(1, n, step, 0)

    def crossing(body, own):
        def step(k, _):
            same = jnp.logical_and(z == j, k == y)

            @pl.when(jnp.logical_not(same))
            def _():
                body(k)

            if own is not None:
                @pl.when(same)
                def _():
                    own(k)

            return 0

        lax.fori_loop(0, ny, step, 0)

    def remote(src, dst, ss, rs, device):
        return pltpu.make_async_remote_copy(
            src_ref=src, dst_ref=dst, send_sem=ss, recv_sem=rs, device_id=device, device_id_type=MESH
        )

    small = [
        pltpu.make_async_copy(source, target, in_s.at[i])
        for i, (source, target) in enumerate(
            ((tok_hbm, tok_ref), (cot_hbm, cot_ref), (routes_hbm, routes_ref), (map_hbm, map_ref), (gates_hbm, gates_ref))
        )
    ]
    for copy in small:
        copy.start()

    barrier = pltpu.get_barrier_semaphore()

    def greet(device):
        pl.semaphore_signal(barrier, inc=1, device_id=device, device_id_type=MESH)

    @pl.when(z != j)
    def _():
        def step(k, _):
            greet(at_t(k))
            return 0

        lax.fori_loop(0, ny, step, 0)

    others(ny, y, lambda k: greet(at_y(k)))
    for k in (2, -2, 1, -1):
        greet(at_z(k))
    others(nx, x_me, lambda k: greet(at_x(k)))
    greet(other_core)
    count = (ny - 1) + 4 + (nx - 1) + 1

    for copy in small:
        copy.wait()
    xs[...] = widen(jnp.concatenate([tok_ref[...].astype(FULL), cot_ref[...].astype(FULL)], axis=0), padded)

    @pl.when(z != j)
    def _():
        pl.semaphore_wait(barrier, count + ny)

    @pl.when(z == j)
    def _():
        pl.semaphore_wait(barrier, count)

    def x_copy(k):
        return remote(xs, xt.at[y], xt_ss.at[k], xt_rs.at[y], at_t(k))

    def x_wait(k):
        return remote(xs, xt.at[k], xt_ss.at[k], xt_rs.at[k], at_t(k))

    def x_own(k):
        xt[k] = xs[...]

    crossing(lambda k: x_copy(k).start(), x_own)

    def columns(k, c):
        return pl.ds(pl.multiple_of(k * quarter + c * BLK, BLK), BLK)

    def band(k):
        return pl.ds(pl.multiple_of(k * rows, 16), rows)

    def w_copies(k, c, slot):
        return [
            remote(ref.at[:, columns(k, c)], wall.at[c, band(slot), pl.ds(i * BLK, BLK)],
                   w_ss.at[c, i, k], w_rs.at[c, i, slot], at_y(k))
            for i, ref in enumerate((gate_ref, up_ref, down_ref))
        ]

    def w_local(c):
        return [
            pltpu.make_async_copy(ref.at[:, columns(y, c)], wall.at[c, band(y), pl.ds(i * BLK, BLK)], wl_s.at[c, i])
            for i, ref in enumerate((gate_ref, up_ref, down_ref))
        ]

    def start_all(copies):
        for copy in copies:
            copy.start()

    def wait_all(copies):
        for copy in copies:
            copy.wait()

    def recv_all(copies):
        for copy in copies:
            copy.wait_recv()

    def send_all(copies):
        for copy in copies:
            copy.wait_send()

    experts = map_ref.shape[1]
    names = lax.broadcasted_iota(jnp.int32, (8, experts), 1)
    named = jnp.zeros((8, experts), FULL)
    for k in range(routes_ref.shape[1]):
        named = named + jnp.where(routes_ref[:, k : k + 1] == names, gates_ref[:, k : k + 1], 0.0)
    picks = [map_ref[pl.ds(j * per + q, 1), :] - j * (ny * nc) for q in range(per)]
    for k in range(ny):
        for c in range(nc):
            takes = sum((pick == k * nc + c).astype(FULL) for pick in picks)
            weight = jnp.sum(named * takes, axis=1, keepdims=True)
            wts[k, :, c * BLK : (c + 1) * BLK] = jnp.broadcast_to(weight, (8, BLK))

    def wt_copy(k):
        return remote(wts.at[k], wbuf.at[y], wt_ss.at[k], wt_rs.at[y], at_y(k))

    def wt_wait(k):
        return remote(wts.at[k], wbuf.at[k], wt_ss.at[k], wt_rs.at[k], at_y(k))

    others(ny, y, lambda k: wt_copy(k).start())
    wbuf[y] = wts[y]

    others(ny, y, lambda k: start_all(w_copies(k, 0, y)))

    crossing(lambda k: x_wait(k).wait_recv(), None)
    landed = xt[...].astype(FULL)[:, :, :feats]
    xb[j] = jnp.concatenate(
        [landed[:, :8].reshape(group, feats), landed[:, 8:].reshape(group, feats)], axis=1
    ).astype(HALF)

    def xb_copy(k, slot):
        return remote(xb.at[slot], xb.at[slot], xb_ss.at[k], xb_rs.at[slot], at_x(k))

    def xc_copy(k, side):
        slot = 2 * k + side
        return remote(xb.at[slot], xb.at[slot], xc_ss.at[k], xb_rs.at[slot], other_core)

    others(nx, x_me, lambda k: xb_copy(k, j).start())
    xc_copy(x_me, core).start()
    for c in range(1, nc):
        others(ny, y, lambda k: start_all(w_copies(k, c, y)))
    for c in range(nc):
        start_all(w_local(c))

    def forward(k):
        xb_copy(k, 2 * k + core).wait_recv()
        xc_copy(k, core).start()

    for k in sorted(range(1, nx), key=lambda k: min(k, nx - k)):
        forward(lax.rem(x_me + k, nx))

    def from_core(k, _):
        xc_copy(k, 1 - core).wait_recv()
        return 0

    lax.fori_loop(0, nx, from_core, 0)
    dyb[...] = xb[:, :, feats:].reshape(tokens_all, feats)

    def x_all():
        return xb[:, :, :feats].reshape(tokens_all, feats)

    def place(k):
        return lax.rem(z + k + nz, nz)

    RS_TO = (-2, 1, -1, -2, 2, -1, 1)

    def rs_copy(c, i):
        return remote(rs_buf.at[c, i], rs_recv.at[c, i], r_ss.at[c, i], r_rs.at[c, i], at_z(RS_TO[i]))

    def rs_send(c, i, target, *arrived):
        value = part[c, place(target)]
        for k in arrived:
            rs_copy(c, k).wait_recv()
            value = value + rs_recv[c, k].astype(FULL)
        rs_buf[c, i] = value.astype(HALF)
        rs_copy(c, i).start()

    AG_TO = (2, -2, 1, -1, 2, 1, -1)
    AG_FROM = (0, 0, 0, 0, -2, -2, 2)

    def ag_copy(c, i, arriving=False):
        origin = place(AG_FROM[i] - AG_TO[i]) if arriving else place(AG_FROM[i])
        return remote(ag.at[c, origin], ag.at[c, origin], a_ss.at[c, i], a_rs.at[c, i], at_z(AG_TO[i]))

    def g_copies(k, c, slot):
        return [
            remote(grads.at[c, band(k), pl.ds(i * BLK, BLK)], ref.at[:, columns(slot, c)],
                   g_ss.at[c, i, k], g_rs.at[c, i, slot], at_y(k))
            for i, ref in enumerate((gate_out, up_out, down_out))
        ]

    def g_local(c):
        return [
            pltpu.make_async_copy(grads.at[c, band(y), pl.ds(i * BLK, BLK)], ref.at[:, columns(y, c)], own_s.at[c, i])
            for i, ref in enumerate((gate_out, up_out, down_out))
        ]

    def first(c):
        wait_all(w_local(c))
        others(ny, y, lambda k: recv_all(w_copies(k, c, k)))
        part[c, :, :, 0 : 2 * BLK] = contract(x_all(), wall[c, :, 0 : 2 * BLK], 1, 0).reshape(nz, group, 2 * BLK)
        part[c, :, :, 2 * BLK : 3 * BLK] = contract(dyb[...], wall[c, :, 2 * BLK : 3 * BLK], 1, 0).reshape(nz, group, BLK)
        rs_send(c, 0, -4)
        rs_send(c, 1, 3)
        rs_send(c, 2, -3)
        rs_send(c, 5, -1)
        rs_send(c, 6, 1)

    def middle(c):
        if c == 0:
            others(ny, y, lambda k: wt_wait(k).wait_recv())
        total = part[c, z]
        for i in (5, 6, 4, 3):
            rs_copy(c, i).wait_recv()
            total = total + rs_recv[c, i].astype(FULL)
        gate_pre, up_pre, hidden_grad = total[:, :BLK], total[:, BLK : 2 * BLK], total[:, 2 * BLK :]
        weight = wbuf[:, :, c * BLK : (c + 1) * BLK].reshape(group, BLK)
        sigma = jax.nn.sigmoid(gate_pre)
        silu = gate_pre * sigma
        scaled = weight * hidden_grad
        ag[c, z, :, 0:BLK] = (scaled * up_pre * sigma * (1.0 + gate_pre * (1.0 - sigma))).astype(HALF)
        ag[c, z, :, BLK : 2 * BLK] = (scaled * silu).astype(HALF)
        ag[c, z, :, 2 * BLK : 3 * BLK] = (weight * silu * up_pre).astype(HALF)
        for i in range(4):
            ag_copy(c, i).start()

    def last(c):
        pair = ag[c, :, :, 0 : 2 * BLK].reshape(tokens_all, 2 * BLK)
        hidden = ag[c, :, :, 2 * BLK : 3 * BLK].reshape(tokens_all, BLK)

        def block_grads():
            grads[c, :, 0 : 2 * BLK] = contract(xtr[...], pair, 1, 0).astype(HALF)
            grads[c, :, 2 * BLK : 3 * BLK] = contract(dytr[...], hidden, 1, 0).astype(HALF)
            others(ny, y, lambda k: start_all(g_copies(k, c, y)))
            start_all(g_local(c))

        if c < nc - 1:
            block_grads()
        out_part = contract(hidden, wall[c, :, 2 * BLK : 3 * BLK], 1, 1)
        in_part = contract(pair, wall[c, :, 0 : 2 * BLK], 1, 1)
        if c > 0:
            out_part = out_part + acc[0]
            in_part = in_part + acc[1]
        if c < nc - 1:
            acc[0], acc[1] = out_part, in_part
        else:
            parts = jnp.concatenate([out_part, in_part], axis=1).reshape(nx, 2, group, 2 * feats)
            op_send[...] = parts.astype(HALF)
            for k in sorted(range(1, nx), key=lambda k: -min(k, nx - k)):
                oc_copy(lax.rem(x_me + k, nx)).start()
            oc_copy(x_me).start()
            block_grads()

    def oc_copy(k):
        return remote(op_send.at[k, 1 - core], op_core.at[k], oc_ss.at[k], oc_rs.at[k], other_core)

    def op_copy(k, slot):
        return remote(op_buf.at[k], op_recv.at[slot], o_ss.at[k], o_rs.at[slot], at_x(k))

    def stage(c, s):
        if s == 0:
            first(c)
        elif s == 1:
            rs_send(c, 4, 2, 1)
            rs_send(c, 3, -2, 2, 0)
        elif s == 2:
            middle(c)
        elif s == 3:
            ag_copy(c, 0, True).wait_recv()
            ag_copy(c, 4).start()
            ag_copy(c, 5).start()
            ag_copy(c, 1, True).wait_recv()
            ag_copy(c, 6).start()
        else:
            for i in (2, 3, 5, 6, 4):
                ag_copy(c, i, True).wait_recv()
            last(c)

    stages = 5
    for s in range(stages):
        for c in range(nc):
            stage(c, s)
        if s == 0:
            xtr[...] = x_all().T
            dytr[...] = dyb[...].T

    def pass_on(k):
        oc_copy(k).wait_recv()
        op_buf[k] = (op_send[k, core].astype(FULL) + op_core[k].astype(FULL)).astype(HALF)
        op_copy(k, x_me).start()

    for k in sorted(range(1, nx), key=lambda k: -min(k, nx - k)):
        pass_on(lax.rem(x_me + k, nx))
    oc_copy(x_me).wait_recv()
    op_recv[x_me] = op_core[x_me]
    others(nx, x_me, lambda k: op_copy(k, k).wait_recv())
    summed = jnp.sum(op_recv[...].astype(FULL), axis=0) + op_send[x_me, core].astype(FULL)
    t_send[...] = widen(
        jnp.concatenate(
            [summed[:, :feats].reshape(ny, 8, feats), summed[:, feats:].reshape(ny, 8, feats)], axis=1
        ),
        padded,
    )

    def t_copy(k):
        return remote(t_send.at[k], t_recv.at[y], t_ss.at[k], t_rs.at[y], at_t(k))

    def t_wait(k):
        return remote(t_send.at[k], t_recv.at[k], t_ss.at[k], t_rs.at[k], at_t(k))

    def t_own(k):
        t_recv[k] = t_send[k]

    crossing(lambda k: t_copy(k).start(), t_own)

    for c in range(nc):
        others(ny, y, lambda k: recv_all(g_copies(k, c, k)))
    crossing(lambda k: x_copy(k).wait_send(), None)
    others(ny, y, lambda k: wt_copy(k).wait_send())
    others(nx, x_me, lambda k: xb_copy(k, j).wait_send())
    for k in range(nx):
        xc_copy(k, core).wait_send()
        oc_copy(k).wait_send()
    others(nx, x_me, lambda k: op_copy(k, x_me).wait_send())
    for c in range(nc):
        others(ny, y, lambda k: send_all(w_copies(k, c, y)))
        for i in range(nz - 1):
            rs_copy(c, i).wait_send()
            ag_copy(c, i).wait_send()
        others(ny, y, lambda k: send_all(g_copies(k, c, y)))
        wait_all(g_local(c))

    crossing(lambda k: t_wait(k).wait_recv(), None)
    final = jnp.sum(t_recv[...].astype(FULL), axis=0)
    mixed_ref[...] = final[:8, :feats].astype(HALF)
    dtok_ref[...] = final[8:, :feats].astype(HALF)
    crossing(lambda k: t_copy(k).wait_send(), None)


def finish(mixed_ref, dtok_ref, gate_ref, up_ref, down_ref, mixed_out, dtok_out, gate_out, up_out, down_out,
           small, halves, fulls, in_s, out_s):
    _, steps, _, width = halves.shape
    moved = [
        (pltpu.make_async_copy(source, small.at[i], in_s.at[i, 0]), pltpu.make_async_copy(small.at[i], target, out_s.at[i, 0]))
        for i, (source, target) in enumerate(((mixed_ref, mixed_out), (dtok_ref, dtok_out)))
    ]
    wide = [(gate_ref, gate_out), (up_ref, up_out), (down_ref, down_out)]

    def load(i, k):
        return pltpu.make_async_copy(wide[i][0].at[:, pl.ds(k * width, width)], halves.at[i, k], in_s.at[2 + i, k])

    def store(i, k):
        return pltpu.make_async_copy(fulls.at[i, k], wide[i][1].at[:, pl.ds(k * width, width)], out_s.at[2 + i, k])

    parts = [(i, k) for i in range(3) for k in range(steps)]
    for i, k in parts:
        load(i, k).start()
    for source, _ in moved:
        source.start()
    for i, k in parts:
        load(i, k).wait()
        fulls[i, k] = halves[i, k].astype(FULL)
        store(i, k).start()
    for source, target in moved:
        source.wait()
        target.start()
    for _, target in moved:
        target.wait()
    for i, k in parts:
        store(i, k).wait()


def shards(tokens, d_out, gate_dense, up_dense, down_dense, block_map, routes, route_gates):
    nj = lax.axis_size("dp")
    ny = lax.axis_size("expert") // nj
    nx = nj // 2
    per = block_map.shape[1] // nj
    rows, width = gate_dense.shape
    tok, feats = tokens.shape
    nc = width // BLK // ny
    group = tok * ny
    padded = -(-feats // BLK) * BLK
    hops = nj - 1
    dma = pltpu.SemaphoreType.DMA
    vmem = pl.BlockSpec(memory_space=pltpu.VMEM)
    hbm = pl.BlockSpec(memory_space=pltpu.HBM)
    outs = (
        jax.ShapeDtypeStruct((tok, feats), HALF),
        jax.ShapeDtypeStruct((tok, feats), HALF),
    ) + (jax.ShapeDtypeStruct((rows, width), HALF),) * 3
    results = pl.pallas_call(
        functools.partial(kernel, nj, ny, nc, per),
        out_shape=outs,
        in_specs=[hbm] * 8,
        out_specs=(vmem,) * 2 + (hbm,) * 3,
        scratch_shapes=[
            pltpu.VMEM((2 * tok, padded), HALF),
            pltpu.VMEM((ny, 2 * tok, padded), HALF),
            pltpu.VMEM((nj, group, 2 * feats), HALF),
            pltpu.VMEM((nj * group, feats), HALF),
            pltpu.VMEM((feats, nj * group), HALF),
            pltpu.VMEM((feats, nj * group), HALF),
            pltpu.VMEM((ny, tok, nc * BLK), FULL),
            pltpu.VMEM((ny, tok, nc * BLK), FULL),
            pltpu.VMEM((nc, ny * rows, 3 * BLK), HALF),
            pltpu.VMEM((nc, nj, group, 3 * BLK), FULL),
            pltpu.VMEM((nc, hops, group, 3 * BLK), HALF),
            pltpu.VMEM((nc, hops, group, 3 * BLK), HALF),
            pltpu.VMEM((nc, nj, group, 3 * BLK), HALF),
            pltpu.VMEM((nc, ny * rows, 3 * BLK), HALF),
            pltpu.VMEM((2, nj * group, feats), FULL),
            pltpu.VMEM((nx, 2, group, 2 * feats), HALF),
            pltpu.VMEM((nx, group, 2 * feats), HALF),
            pltpu.VMEM((nx, group, 2 * feats), HALF),
            pltpu.VMEM((nx, group, 2 * feats), HALF),
            pltpu.VMEM((ny, 2 * tok, padded), HALF),
            pltpu.VMEM((ny, 2 * tok, padded), HALF),
            pltpu.VMEM((tok, feats), HALF),
            pltpu.VMEM((tok, feats), HALF),
            pltpu.VMEM(routes.shape, jnp.int32),
            pltpu.VMEM(block_map.shape[::-1], jnp.int32),
            pltpu.VMEM((1, routes.shape[1]), FULL),
            dma((5,)), dma((nc, 3)),
            dma((ny,)), dma((ny,)), dma((nx,)), dma((nj,)), dma((nx,)),
            dma((ny,)), dma((ny,)), dma((nc, 3)),
            dma((nc, 3, ny)), dma((nc, 3, ny)),
            dma((nc, hops)), dma((nc, hops)), dma((nc, hops)), dma((nc, hops)),
            dma((nc, 3, ny)), dma((nc, 3, ny)),
            dma((nx,)), dma((nx,)), dma((nx,)), dma((nx,)), dma((ny,)), dma((ny,)),
        ],
        compiler_params=pltpu.CompilerParams(
            collective_id=0, has_side_effects=True, vmem_limit_bytes=LIMIT
        ),
    )(tokens, d_out, routes, block_map.T, route_gates.reshape(1, -1), gate_dense, up_dense, down_dense.T)
    steps = 2
    mixed, d_tokens, gate_grad, up_grad, down_grad = pl.pallas_call(
        finish,
        out_shape=outs[:2] + (jax.ShapeDtypeStruct((rows, width), FULL),) * 3,
        in_specs=[hbm] * 5,
        out_specs=(hbm,) * 5,
        scratch_shapes=[
            pltpu.VMEM((2, tok, feats), HALF),
            pltpu.VMEM((3, steps, rows, width // steps), HALF),
            pltpu.VMEM((3, steps, rows, width // steps), FULL),
            dma((5, steps)),
            dma((5, steps)),
        ],
        compiler_params=pltpu.CompilerParams(vmem_limit_bytes=LIMIT),
    )(*results)
    return mixed, d_tokens, gate_grad, up_grad, down_grad.T


def solution(mesh):
    in_specs = (
        P("expert", "dp"),
        P("expert", "dp"),
        P("expert", "dp"),
        P("expert", "dp"),
        P("dp", "expert"),
        P(),
        P("expert", None),
        P(),
    )
    out_specs = (
        P("expert", "dp"),
        P("expert", "dp"),
        P("expert", "dp"),
        P("expert", "dp"),
        P("dp", "expert"),
    )
    return jax.shard_map(shards, mesh=mesh, in_specs=in_specs, out_specs=out_specs, check_vma=False)
```

```python
import functools

import jax
import jax.numpy as jnp
from jax import lax
from jax.experimental import pallas as pl
from jax.experimental.pallas import tpu as pltpu
from jax.sharding import PartitionSpec as P

BLK = 128
MESH = pl.DeviceIdType.MESH
LIMIT = 60 * 1024 * 1024
ORDER = "f0 f1 f2 t0 a0 a1 a2 m0 m1 m2 b0 b1 b2 r0 g0 o0 r1 g1 o1 r2 o2 g2"
HALF, FULL = jnp.bfloat16, jnp.float32


def contract(left, right, left_dim, right_dim):
    return lax.dot_general(left, right, (((left_dim,), (right_dim,)), ((), ())), preferred_element_type=FULL)


def widen(rows, lanes):
    fill = jnp.zeros(rows.shape[:-1] + (lanes - rows.shape[-1],), rows.dtype)
    return jnp.concatenate([rows, fill], axis=-1).astype(HALF)


def kernel(
    nj, ny, nc, per,
    tok_hbm, cot_hbm, routes_hbm, map_hbm, gates_hbm, gate_ref, up_ref, down_ref,
    mixed_ref, dtok_ref, gate_out, up_out, down_out,
    xs, xt, xb, dyb, xtr, dytr, wts, wbuf, wall, part, rs_buf, rs_recv, ag, grads, acc,
    op_send, op_core, op_buf, op_recv, t_send, t_recv,
    tok_ref, cot_ref, routes_ref, map_ref, gates_ref, in_s, own_s,
    xt_ss, xt_rs, xb_ss, xb_rs, xc_ss, wt_ss, wt_rs, wl_s, w_ss, w_rs, r_ss, r_rs, a_ss, a_rs, g_ss, g_rs,
    oc_ss, oc_rs, o_ss, o_rs, t_ss, t_rs,
):
    nz, nx = nj, nj // 2
    j = lax.axis_index("dp")
    e = lax.axis_index("expert")
    x_me, core = j // 2, lax.rem(j, 2)
    z, y = e // ny, lax.rem(e, ny)
    rows = gate_ref.shape[0]
    quarter = gate_ref.shape[1] // ny
    feats, padded = tok_hbm.shape[1], xs.shape[1]
    group = 8 * ny
    tokens_all = nj * group

    def at_y(k):
        return (j, z * ny + k)

    def at_z(k):
        return (j, lax.rem(z + k + nz, nz) * ny + y)

    def at_x(k):
        return (2 * k + core, e)

    def pick(values, index):
        return sum(jnp.where(index == i, value, 0) for i, value in enumerate(values))

    def slot_of(device):
        ahead = lax.rem(device // 2 - z // 2 + nx, nx)
        return lax.rem(z + pick((4, 3, 5, 2, 1, 0, 6, 7), 2 * ahead + lax.rem(device, 2)), nz)

    mine = slot_of(j)
    ahead = lax.rem(z - j + nz, nz)
    keeper = 2 * lax.rem(j // 2 + pick((2, 2, 1, 0, 0, 1, 3, 3), ahead), nx) + pick((1, 0, 1, 1, 0, 0, 0, 1), ahead)

    def at_keeper(k):
        return (keeper, j * ny + k)

    def at_source(k):
        return (z, mine * ny + k)

    other_core = (2 * x_me + 1 - core, e)

    def others(n, me, body):
        def step(i, _):
            body(lax.rem(me + i, n))
            return 0

        lax.fori_loop(1, n, step, 0)

    def each_y(body):
        def step(k, _):
            body(k)
            return 0

        lax.fori_loop(0, ny, step, 0)

    def remote(src, dst, ss, rs, device):
        return pltpu.make_async_remote_copy(
            src_ref=src, dst_ref=dst, send_sem=ss, recv_sem=rs, device_id=device, device_id_type=MESH
        )

    small = [
        pltpu.make_async_copy(source, target, in_s.at[i])
        for i, (source, target) in enumerate(
            ((tok_hbm, tok_ref), (cot_hbm, cot_ref), (routes_hbm, routes_ref), (map_hbm, map_ref), (gates_hbm, gates_ref))
        )
    ]
    for copy in small:
        copy.start()

    barrier = pltpu.get_barrier_semaphore()

    def greet(device):
        pl.semaphore_signal(barrier, inc=1, device_id=device, device_id_type=MESH)

    each_y(lambda k: greet(at_keeper(k)))
    each_y(lambda k: greet(at_source(k)))
    others(ny, y, lambda k: greet(at_y(k)))
    for k in (2, -2, 1, -1):
        greet(at_z(k))
    others(nx, x_me, lambda k: greet(at_x(k)))
    greet(other_core)
    count = 2 * ny + (ny - 1) + 4 + (nx - 1) + 1

    for copy in small:
        copy.wait()
    xs[...] = widen(jnp.concatenate([tok_ref[...].astype(FULL), cot_ref[...].astype(FULL)], axis=0), padded)

    pl.semaphore_wait(barrier, count)

    def x_copy(k):
        return remote(xs, xt.at[y], xt_ss.at[k], xt_rs.at[y], at_keeper(k))

    def x_wait(k):
        return remote(xs, xt.at[k], xt_ss.at[k], xt_rs.at[k], at_source(k))

    each_y(lambda k: x_copy(k).start())

    def columns(k, c):
        return pl.ds(pl.multiple_of(k * quarter + c * BLK, BLK), BLK)

    def band(k):
        return pl.ds(pl.multiple_of(k * rows, 16), rows)

    def w_copies(k, c, slot):
        return [
            remote(ref.at[:, columns(k, c)], wall.at[c, band(slot), pl.ds(i * BLK, BLK)],
                   w_ss.at[c, i, k], w_rs.at[c, i, slot], at_y(k))
            for i, ref in enumerate((gate_ref, up_ref, down_ref))
        ]

    def w_local(c):
        return [
            pltpu.make_async_copy(ref.at[:, columns(y, c)], wall.at[c, band(y), pl.ds(i * BLK, BLK)], wl_s.at[c, i])
            for i, ref in enumerate((gate_ref, up_ref, down_ref))
        ]

    def start_all(copies):
        for copy in copies:
            copy.start()

    def wait_all(copies):
        for copy in copies:
            copy.wait()

    def recv_all(copies):
        for copy in copies:
            copy.wait_recv()

    def send_all(copies):
        for copy in copies:
            copy.wait_send()

    experts = map_ref.shape[1]
    names = lax.broadcasted_iota(jnp.int32, (8, experts), 1)
    named = jnp.zeros((8, experts), FULL)
    for k in range(routes_ref.shape[1]):
        named = named + jnp.where(routes_ref[:, k : k + 1] == names, gates_ref[:, k : k + 1], 0.0)
    picks = [map_ref[pl.ds(j * per + q, 1), :] - j * (ny * nc) for q in range(per)]
    for k in range(ny):
        for c in range(nc):
            takes = sum((pick == k * nc + c).astype(FULL) for pick in picks)
            weight = jnp.sum(named * takes, axis=1, keepdims=True)
            wts[k, :, c * BLK : (c + 1) * BLK] = jnp.broadcast_to(weight, (8, BLK))

    def wt_copy(k):
        return remote(wts.at[k], wbuf.at[y], wt_ss.at[k], wt_rs.at[y], at_y(k))

    def wt_wait(k):
        return remote(wts.at[k], wbuf.at[k], wt_ss.at[k], wt_rs.at[k], at_y(k))

    others(ny, y, lambda k: wt_copy(k).start())
    wbuf[y] = wts[y]

    others(ny, y, lambda k: start_all(w_copies(k, 0, y)))

    each_y(lambda k: x_wait(k).wait_recv())
    landed = xt[...].astype(FULL)[:, :, :feats]
    xb[mine] = jnp.concatenate(
        [landed[:, :8].reshape(group, feats), landed[:, 8:].reshape(group, feats)], axis=1
    ).astype(HALF)

    def xb_copy(k, slot):
        return remote(xb.at[slot], xb.at[slot], xb_ss.at[k], xb_rs.at[slot], at_x(k))

    def xc_copy(k, side):
        slot = slot_of(2 * k + side)
        return remote(xb.at[slot], xb.at[slot], xc_ss.at[k], xb_rs.at[slot], other_core)

    others(nx, x_me, lambda k: xb_copy(k, mine).start())
    xc_copy(x_me, core).start()
    for c in range(1, nc):
        others(ny, y, lambda k: start_all(w_copies(k, c, y)))
    for c in range(nc):
        start_all(w_local(c))

    def forward(k):
        xb_copy(k, slot_of(2 * k + core)).wait_recv()
        xc_copy(k, core).start()

    for k in sorted(range(1, nx), key=lambda k: min(k, nx - k)):
        forward(lax.rem(x_me + k, nx))

    def from_core(k, _):
        xc_copy(k, 1 - core).wait_recv()
        return 0

    lax.fori_loop(0, nx, from_core, 0)
    dyb[...] = xb[:, :, feats:].reshape(tokens_all, feats)

    def x_all():
        return xb[:, :, :feats].reshape(tokens_all, feats)

    def place(k):
        return lax.rem(z + k + nz, nz)

    cut = group // 2
    low, high, both = pl.ds(0, cut), pl.ds(cut, cut), pl.ds(0, group)
    RS_TO = (-2, 1, -1, -2, 2, -1, 1, 2)
    RS_ROWS = (low, both, both, both, both, both, both, high)

    def rs_copy(c, i):
        return remote(rs_buf.at[c, i, RS_ROWS[i], :], rs_recv.at[c, i, RS_ROWS[i], :],
                      r_ss.at[c, i], r_rs.at[c, i], at_z(RS_TO[i]))

    def rs_send(c, i, target, piece=None, half=None):
        value = part[c, place(target)]
        if piece is not None:
            rs_copy(c, half).wait_recv()
            rs_copy(c, piece).wait_recv()
            value = value + rs_recv[c, piece].astype(FULL)
            extra = rs_recv[c, half, RS_ROWS[half], :].astype(FULL)
            if half == 0:
                value = jnp.concatenate([value[:cut] + extra, value[cut:]], axis=0)
            else:
                value = jnp.concatenate([value[:cut], value[cut:] + extra], axis=0)
        rs_buf[c, i] = value.astype(HALF)
        rs_copy(c, i).start()

    AG_TO = (2, -2, 1, -1, 2, 1, -1, -2)
    AG_FROM = (0, 0, 0, 0, -2, -2, 2, 2)
    AG_ROWS = (both, both, both, both, low, both, both, high)

    def ag_copy(c, i, arriving=False):
        origin = place(AG_FROM[i] - AG_TO[i]) if arriving else place(AG_FROM[i])
        piece = ag.at[c, origin, AG_ROWS[i], :]
        return remote(piece, piece, a_ss.at[c, i], a_rs.at[c, i], at_z(AG_TO[i]))

    def g_copies(k, c, slot):
        return [
            remote(grads.at[c, band(k), pl.ds(i * BLK, BLK)], ref.at[:, columns(slot, c)],
                   g_ss.at[c, i, k], g_rs.at[c, i, slot], at_y(k))
            for i, ref in enumerate((gate_out, up_out, down_out))
        ]

    def g_local(c):
        return [
            pltpu.make_async_copy(grads.at[c, band(y), pl.ds(i * BLK, BLK)], ref.at[:, columns(y, c)], own_s.at[c, i])
            for i, ref in enumerate((gate_out, up_out, down_out))
        ]

    def first(c):
        wait_all(w_local(c))
        others(ny, y, lambda k: recv_all(w_copies(k, c, k)))
        part[c, :, :, 0 : 2 * BLK] = contract(x_all(), wall[c, :, 0 : 2 * BLK], 1, 0).reshape(nz, group, 2 * BLK)
        part[c, :, :, 2 * BLK : 3 * BLK] = contract(dyb[...], wall[c, :, 2 * BLK : 3 * BLK], 1, 0).reshape(nz, group, BLK)
        rs_send(c, 0, 4)
        rs_send(c, 7, 4)
        rs_send(c, 1, 3)
        rs_send(c, 2, -3)
        rs_send(c, 5, -1)
        rs_send(c, 6, 1)

    def middle(c):
        if c == 0:
            others(ny, y, lambda k: wt_wait(k).wait_recv())
        total = part[c, z]
        for i in (5, 6, 4, 3):
            rs_copy(c, i).wait_recv()
            total = total + rs_recv[c, i].astype(FULL)
        gate_pre, up_pre, hidden_grad = total[:, :BLK], total[:, BLK : 2 * BLK], total[:, 2 * BLK :]
        weight = wbuf[:, :, c * BLK : (c + 1) * BLK].reshape(group, BLK)
        sigma = jax.nn.sigmoid(gate_pre)
        silu = gate_pre * sigma
        scaled = weight * hidden_grad
        ag[c, z, :, 0:BLK] = (scaled * up_pre * sigma * (1.0 + gate_pre * (1.0 - sigma))).astype(HALF)
        ag[c, z, :, BLK : 2 * BLK] = (scaled * silu).astype(HALF)
        ag[c, z, :, 2 * BLK : 3 * BLK] = (weight * silu * up_pre).astype(HALF)
        for i in range(4):
            ag_copy(c, i).start()

    def halves(c):
        pair = ag[c, :, :, 0 : 2 * BLK].reshape(tokens_all, 2 * BLK)
        return pair, ag[c, :, :, 2 * BLK : 3 * BLK].reshape(tokens_all, BLK)

    def block_grads(c):
        pair, hidden = halves(c)
        grads[c, :, 0 : 2 * BLK] = contract(xtr[...], pair, 1, 0).astype(HALF)
        grads[c, :, 2 * BLK : 3 * BLK] = contract(dytr[...], hidden, 1, 0).astype(HALF)
        others(ny, y, lambda k: start_all(g_copies(k, c, y)))
        start_all(g_local(c))

    def outputs(c):
        pair, hidden = halves(c)
        out_part = contract(hidden, wall[c, :, 2 * BLK : 3 * BLK], 1, 1)
        in_part = contract(pair, wall[c, :, 0 : 2 * BLK], 1, 1)
        if c > 0:
            out_part = out_part + acc[0]
            in_part = in_part + acc[1]
        if c < nc - 1:
            acc[0], acc[1] = out_part, in_part
        else:
            parts = jnp.concatenate([out_part, in_part], axis=1).reshape(nj, group, 2 * feats)
            op_send[...] = parts.astype(HALF)
            for k in sorted(range(1, nx), key=lambda k: -min(k, nx - k)):
                oc_copy(lax.rem(x_me + k, nx)).start()
            oc_copy(x_me).start()

    def oc_copy(k):
        return remote(op_send.at[slot_of(2 * k + 1 - core)], op_core.at[k], oc_ss.at[k], oc_rs.at[k], other_core)

    def op_copy(k, slot):
        return remote(op_buf.at[k], op_recv.at[slot], o_ss.at[k], o_rs.at[slot], at_x(k))

    def second(c):
        rs_send(c, 4, 2, 1, 7)
        rs_send(c, 3, -2, 2, 0)

    def onward(c):
        ag_copy(c, 0, True).wait_recv()
        ag_copy(c, 4).start()
        ag_copy(c, 5).start()
        ag_copy(c, 1, True).wait_recv()
        ag_copy(c, 6).start()
        ag_copy(c, 7).start()

    def arrived(c):
        for i in (2, 3, 5, 6, 4, 7):
            ag_copy(c, i, True).wait_recv()

    def turned(c):
        xtr[...] = x_all().T
        dytr[...] = dyb[...].T

    steps = dict(f=first, a=second, m=middle, b=onward, r=arrived, g=block_grads, o=outputs, t=turned)
    for step in ORDER.split():
        steps[step[0]](int(step[1]))

    def pass_on(k):
        oc_copy(k).wait_recv()
        op_buf[k] = (op_send[slot_of(2 * k + core)].astype(FULL) + op_core[k].astype(FULL)).astype(HALF)
        op_copy(k, x_me).start()

    for k in sorted(range(1, nx), key=lambda k: -min(k, nx - k)):
        pass_on(lax.rem(x_me + k, nx))
    oc_copy(x_me).wait_recv()
    op_recv[x_me] = op_core[x_me]
    others(nx, x_me, lambda k: op_copy(k, k).wait_recv())
    summed = jnp.sum(op_recv[...].astype(FULL), axis=0) + op_send[mine].astype(FULL)
    t_send[...] = widen(
        jnp.concatenate(
            [summed[:, :feats].reshape(ny, 8, feats), summed[:, feats:].reshape(ny, 8, feats)], axis=1
        ),
        padded,
    )

    def t_copy(k):
        return remote(t_send.at[k], t_recv.at[y], t_ss.at[k], t_rs.at[y], at_source(k))

    def t_wait(k):
        return remote(t_send.at[k], t_recv.at[k], t_ss.at[k], t_rs.at[k], at_keeper(k))

    each_y(lambda k: t_copy(k).start())

    for c in range(nc):
        others(ny, y, lambda k: recv_all(g_copies(k, c, k)))
    each_y(lambda k: x_copy(k).wait_send())
    others(ny, y, lambda k: wt_copy(k).wait_send())
    others(nx, x_me, lambda k: xb_copy(k, mine).wait_send())
    for k in range(nx):
        xc_copy(k, core).wait_send()
        oc_copy(k).wait_send()
    others(nx, x_me, lambda k: op_copy(k, x_me).wait_send())
    for c in range(nc):
        others(ny, y, lambda k: send_all(w_copies(k, c, y)))
        for i in range(nz):
            rs_copy(c, i).wait_send()
            ag_copy(c, i).wait_send()
        others(ny, y, lambda k: send_all(g_copies(k, c, y)))
        wait_all(g_local(c))

    each_y(lambda k: t_wait(k).wait_recv())
    final = jnp.sum(t_recv[...].astype(FULL), axis=0)
    mixed_ref[...] = final[:8, :feats].astype(HALF)
    dtok_ref[...] = final[8:, :feats].astype(HALF)
    each_y(lambda k: t_copy(k).wait_send())


def finish(mixed_ref, dtok_ref, gate_ref, up_ref, down_ref, mixed_out, dtok_out, gate_out, up_out, down_out,
           small, halves, fulls, in_s, out_s):
    _, steps, _, width = halves.shape
    moved = [
        (pltpu.make_async_copy(source, small.at[i], in_s.at[i, 0]), pltpu.make_async_copy(small.at[i], target, out_s.at[i, 0]))
        for i, (source, target) in enumerate(((mixed_ref, mixed_out), (dtok_ref, dtok_out)))
    ]
    wide = [(gate_ref, gate_out), (up_ref, up_out), (down_ref, down_out)]

    def load(i, k):
        return pltpu.make_async_copy(wide[i][0].at[:, pl.ds(k * width, width)], halves.at[i, k], in_s.at[2 + i, k])

    def store(i, k):
        return pltpu.make_async_copy(fulls.at[i, k], wide[i][1].at[:, pl.ds(k * width, width)], out_s.at[2 + i, k])

    parts = [(i, k) for i in range(3) for k in range(steps)]
    for i, k in parts:
        load(i, k).start()
    for source, _ in moved:
        source.start()
    for i, k in parts:
        load(i, k).wait()
        fulls[i, k] = halves[i, k].astype(FULL)
        store(i, k).start()
    for source, target in moved:
        source.wait()
        target.start()
    for _, target in moved:
        target.wait()
    for i, k in parts:
        store(i, k).wait()


def shards(tokens, d_out, gate_dense, up_dense, down_dense, block_map, routes, route_gates):
    nj = lax.axis_size("dp")
    ny = lax.axis_size("expert") // nj
    nx = nj // 2
    per = block_map.shape[1] // nj
    rows, width = gate_dense.shape
    tok, feats = tokens.shape
    nc = width // BLK // ny
    group = tok * ny
    padded = -(-feats // BLK) * BLK
    dma = pltpu.SemaphoreType.DMA
    vmem = pl.BlockSpec(memory_space=pltpu.VMEM)
    hbm = pl.BlockSpec(memory_space=pltpu.HBM)
    outs = (
        jax.ShapeDtypeStruct((tok, feats), HALF),
        jax.ShapeDtypeStruct((tok, feats), HALF),
    ) + (jax.ShapeDtypeStruct((rows, width), HALF),) * 3
    results = pl.pallas_call(
        functools.partial(kernel, nj, ny, nc, per),
        out_shape=outs,
        in_specs=[hbm] * 8,
        out_specs=(vmem,) * 2 + (hbm,) * 3,
        scratch_shapes=[
            pltpu.VMEM((2 * tok, padded), HALF),
            pltpu.VMEM((ny, 2 * tok, padded), HALF),
            pltpu.VMEM((nj, group, 2 * feats), HALF),
            pltpu.VMEM((nj * group, feats), HALF),
            pltpu.VMEM((feats, nj * group), HALF),
            pltpu.VMEM((feats, nj * group), HALF),
            pltpu.VMEM((ny, tok, nc * BLK), FULL),
            pltpu.VMEM((ny, tok, nc * BLK), FULL),
            pltpu.VMEM((nc, ny * rows, 3 * BLK), HALF),
            pltpu.VMEM((nc, nj, group, 3 * BLK), FULL),
            pltpu.VMEM((nc, nj, group, 3 * BLK), HALF),
            pltpu.VMEM((nc, nj, group, 3 * BLK), HALF),
            pltpu.VMEM((nc, nj, group, 3 * BLK), HALF),
            pltpu.VMEM((nc, ny * rows, 3 * BLK), HALF),
            pltpu.VMEM((2, nj * group, feats), FULL),
            pltpu.VMEM((nj, group, 2 * feats), HALF),
            pltpu.VMEM((nx, group, 2 * feats), HALF),
            pltpu.VMEM((nx, group, 2 * feats), HALF),
            pltpu.VMEM((nx, group, 2 * feats), HALF),
            pltpu.VMEM((ny, 2 * tok, padded), HALF),
            pltpu.VMEM((ny, 2 * tok, padded), HALF),
            pltpu.VMEM((tok, feats), HALF),
            pltpu.VMEM((tok, feats), HALF),
            pltpu.VMEM(routes.shape, jnp.int32),
            pltpu.VMEM(block_map.shape[::-1], jnp.int32),
            pltpu.VMEM((1, routes.shape[1]), FULL),
            dma((5,)), dma((nc, 3)),
            dma((ny,)), dma((ny,)), dma((nx,)), dma((nj,)), dma((nx,)),
            dma((ny,)), dma((ny,)), dma((nc, 3)),
            dma((nc, 3, ny)), dma((nc, 3, ny)),
            dma((nc, nj)), dma((nc, nj)), dma((nc, nj)), dma((nc, nj)),
            dma((nc, 3, ny)), dma((nc, 3, ny)),
            dma((nx,)), dma((nx,)), dma((nx,)), dma((nx,)), dma((ny,)), dma((ny,)),
        ],
        compiler_params=pltpu.CompilerParams(
            collective_id=0, has_side_effects=True, vmem_limit_bytes=LIMIT
        ),
    )(tokens, d_out, routes, block_map.T, route_gates.reshape(1, -1), gate_dense, up_dense, down_dense.T)
    steps = 2
    mixed, d_tokens, gate_grad, up_grad, down_grad = pl.pallas_call(
        finish,
        out_shape=outs[:2] + (jax.ShapeDtypeStruct((rows, width), FULL),) * 3,
        in_specs=[hbm] * 5,
        out_specs=(hbm,) * 5,
        scratch_shapes=[
            pltpu.VMEM((2, tok, feats), HALF),
            pltpu.VMEM((3, steps, rows, width // steps), HALF),
            pltpu.VMEM((3, steps, rows, width // steps), FULL),
            dma((5, steps)),
            dma((5, steps)),
        ],
        compiler_params=pltpu.CompilerParams(vmem_limit_bytes=LIMIT),
    )(*results)
    return mixed, d_tokens, gate_grad, up_grad, down_grad.T


def solution(mesh):
    in_specs = (
        P("expert", "dp"),
        P("expert", "dp"),
        P("expert", "dp"),
        P("expert", "dp"),
        P("dp", "expert"),
        P(),
        P("expert", None),
        P(),
    )
    out_specs = (
        P("expert", "dp"),
        P("expert", "dp"),
        P("expert", "dp"),
        P("expert", "dp"),
        P("dp", "expert"),
    )
    return jax.shard_map(shards, mesh=mesh, in_specs=in_specs, out_specs=out_specs, check_vma=False)
```

```python
import functools

import jax
import jax.numpy as jnp
from jax import lax
from jax.experimental import pallas as pl
from jax.experimental.pallas import tpu as pltpu
from jax.sharding import PartitionSpec as P

BLK = 128
MESH = pl.DeviceIdType.MESH
LIMIT = 60 * 1024 * 1024
HALF, FULL = jnp.bfloat16, jnp.float32


def contract(left, right, left_dim, right_dim):
    return lax.dot_general(left, right, (((left_dim,), (right_dim,)), ((), ())), preferred_element_type=FULL)


def widen(rows, lanes):
    fill = jnp.zeros(rows.shape[:-1] + (lanes - rows.shape[-1],), rows.dtype)
    return jnp.concatenate([rows, fill], axis=-1).astype(HALF)


def kernel(
    nj, ny, nc, per,
    tok_hbm, cot_hbm, routes_hbm, map_hbm, gates_hbm, gate_ref, up_ref, down_ref,
    mixed_ref, dtok_ref, gate_out, up_out, down_out,
    xs, xt, xb, dyb, xtr, dytr, wts, wbuf, wall, part, rs_buf, rs_recv, ag, grads, acc,
    op_send, op_core, op_buf, op_recv, t_send, t_recv,
    tok_ref, cot_ref, routes_ref, map_ref, gates_ref, in_s, own_s,
    xt_ss, xt_rs, xb_ss, xb_rs, xc_ss, wt_ss, wt_rs, wl_s, w_ss, w_rs, r_ss, r_rs, a_ss, a_rs, g_ss, g_rs,
    oc_ss, oc_rs, o_ss, o_rs, t_ss, t_rs,
):
    nz, nx = nj, nj // 2
    j = lax.axis_index("dp")
    e = lax.axis_index("expert")
    x_me, core = j // 2, lax.rem(j, 2)
    z, y = e // ny, lax.rem(e, ny)
    rows = gate_ref.shape[0]
    quarter = gate_ref.shape[1] // ny
    feats, padded = tok_hbm.shape[1], xs.shape[1]
    group = 8 * ny
    tokens_all = nj * group

    def at_y(k):
        return (j, z * ny + k)

    def at_z(k):
        return (j, lax.rem(z + k + nz, nz) * ny + y)

    def at_x(k):
        return (2 * k + core, e)

    def pick(values, index):
        return sum(jnp.where(index == i, value, 0) for i, value in enumerate(values))

    def slot_of(device):
        ahead = lax.rem(device // 2 - z // 2 + nx, nx)
        return lax.rem(z + pick((4, 3, 5, 2, 1, 0, 6, 7), 2 * ahead + lax.rem(device, 2)), nz)

    mine = slot_of(j)
    ahead = lax.rem(z - j + nz, nz)
    keeper = 2 * lax.rem(j // 2 + pick((2, 2, 1, 0, 0, 1, 3, 3), ahead), nx) + pick((1, 0, 1, 1, 0, 0, 0, 1), ahead)

    def at_keeper(k):
        return (keeper, j * ny + k)

    def at_source(k):
        return (z, mine * ny + k)

    other_core = (2 * x_me + 1 - core, e)

    def others(n, me, body):
        for i in sorted(range(1, n), key=lambda i: -min(i, n - i)):
            body(lax.rem(me + i, n))

    def each_y(body):
        def step(k, _):
            body(k)
            return 0

        lax.fori_loop(0, ny, step, 0)

    def remote(src, dst, ss, rs, device):
        return pltpu.make_async_remote_copy(
            src_ref=src, dst_ref=dst, send_sem=ss, recv_sem=rs, device_id=device, device_id_type=MESH
        )

    small = [
        pltpu.make_async_copy(source, target, in_s.at[i])
        for i, (source, target) in enumerate(
            ((tok_hbm, tok_ref), (cot_hbm, cot_ref), (routes_hbm, routes_ref), (map_hbm, map_ref), (gates_hbm, gates_ref))
        )
    ]
    for copy in small:
        copy.start()

    barrier = pltpu.get_barrier_semaphore()

    def greet(device):
        pl.semaphore_signal(barrier, inc=1, device_id=device, device_id_type=MESH)

    each_y(lambda k: greet(at_keeper(k)))
    each_y(lambda k: greet(at_source(k)))
    others(ny, y, lambda k: greet(at_y(k)))
    for k in (2, -2, 1, -1):
        greet(at_z(k))
    others(nx, x_me, lambda k: greet(at_x(k)))
    greet(other_core)
    count = 2 * ny + (ny - 1) + 4 + (nx - 1) + 1

    for copy in small:
        copy.wait()
    xs[...] = widen(jnp.concatenate([tok_ref[...].astype(FULL), cot_ref[...].astype(FULL)], axis=0), padded)

    pl.semaphore_wait(barrier, count)

    def x_copy(k):
        return remote(xs, xt.at[y], xt_ss.at[k], xt_rs.at[y], at_keeper(k))

    def x_wait(k):
        return remote(xs, xt.at[k], xt_ss.at[k], xt_rs.at[k], at_source(k))

    each_y(lambda k: x_copy(k).start())

    def columns(k, c):
        return pl.ds(pl.multiple_of(k * quarter + c * BLK, BLK), BLK)

    def band(k):
        return pl.ds(pl.multiple_of(k * rows, 16), rows)

    def w_copies(k, c, slot):
        return [
            remote(ref.at[:, columns(k, c)], wall.at[c, band(slot), pl.ds(i * BLK, BLK)],
                   w_ss.at[c, i, k], w_rs.at[c, i, slot], at_y(k))
            for i, ref in enumerate((gate_ref, up_ref, down_ref))
        ]

    def w_local(c):
        return [
            pltpu.make_async_copy(ref.at[:, columns(y, c)], wall.at[c, band(y), pl.ds(i * BLK, BLK)], wl_s.at[c, i])
            for i, ref in enumerate((gate_ref, up_ref, down_ref))
        ]

    def start_all(copies):
        for copy in copies:
            copy.start()

    def wait_all(copies):
        for copy in copies:
            copy.wait()

    def recv_all(copies):
        for copy in copies:
            copy.wait_recv()

    def send_all(copies):
        for copy in copies:
            copy.wait_send()

    experts = map_ref.shape[1]
    names = lax.broadcasted_iota(jnp.int32, (8, experts), 1)
    named = jnp.zeros((8, experts), FULL)
    for k in range(routes_ref.shape[1]):
        named = named + jnp.where(routes_ref[:, k : k + 1] == names, gates_ref[:, k : k + 1], 0.0)
    picks = [map_ref[pl.ds(j * per + q, 1), :] - j * (ny * nc) for q in range(per)]
    for k in range(ny):
        for c in range(nc):
            takes = sum((pick == k * nc + c).astype(FULL) for pick in picks)
            weight = jnp.sum(named * takes, axis=1, keepdims=True)
            wts[k, :, c * BLK : (c + 1) * BLK] = jnp.broadcast_to(weight, (8, BLK))

    def wt_copy(k):
        return remote(wts.at[k], wbuf.at[y], wt_ss.at[k], wt_rs.at[y], at_y(k))

    def wt_wait(k):
        return remote(wts.at[k], wbuf.at[k], wt_ss.at[k], wt_rs.at[k], at_y(k))

    others(ny, y, lambda k: wt_copy(k).start())
    wbuf[y] = wts[y]

    others(ny, y, lambda k: start_all(w_copies(k, 0, y)))

    each_y(lambda k: x_wait(k).wait_recv())
    landed = xt[...].astype(FULL)[:, :, :feats]
    xb[mine] = jnp.concatenate(
        [landed[:, :8].reshape(group, feats), landed[:, 8:].reshape(group, feats)], axis=1
    ).astype(HALF)

    def xb_copy(k, slot):
        return remote(xb.at[slot], xb.at[slot], xb_ss.at[k], xb_rs.at[slot], at_x(k))

    def xc_copy(k, side):
        slot = slot_of(2 * k + side)
        return remote(xb.at[slot], xb.at[slot], xc_ss.at[k], xb_rs.at[slot], other_core)

    others(nx, x_me, lambda k: xb_copy(k, mine).start())
    xc_copy(x_me, core).start()
    for c in range(1, nc):
        others(ny, y, lambda k: start_all(w_copies(k, c, y)))
    for c in range(nc):
        start_all(w_local(c))

    def forward(k):
        xb_copy(k, slot_of(2 * k + core)).wait_recv()
        xc_copy(k, core).start()

    for k in sorted(range(1, nx), key=lambda k: min(k, nx - k)):
        forward(lax.rem(x_me + k, nx))

    def from_core(k, _):
        xc_copy(k, 1 - core).wait_recv()
        return 0

    lax.fori_loop(0, nx, from_core, 0)
    dyb[...] = xb[:, :, feats:].reshape(tokens_all, feats)

    def x_all():
        return xb[:, :, :feats].reshape(tokens_all, feats)

    def place(k):
        return lax.rem(z + k + nz, nz)

    cut = group // 2
    low, high, both = pl.ds(0, cut), pl.ds(cut, cut), pl.ds(0, group)
    RS_TO = (-2, 1, -1, -2, 2, -1, 1, 2)
    RS_ROWS = (low, both, both, both, both, both, both, high)

    def rs_copy(c, i):
        return remote(rs_buf.at[c, i, RS_ROWS[i], :], rs_recv.at[c, i, RS_ROWS[i], :],
                      r_ss.at[c, i], r_rs.at[c, i], at_z(RS_TO[i]))

    def rs_send(c, i, target, piece=None, half=None):
        value = part[c, place(target)]
        if piece is not None:
            rs_copy(c, half).wait_recv()
            rs_copy(c, piece).wait_recv()
            value = value + rs_recv[c, piece].astype(FULL)
            extra = rs_recv[c, half, RS_ROWS[half], :].astype(FULL)
            if half == 0:
                value = jnp.concatenate([value[:cut] + extra, value[cut:]], axis=0)
            else:
                value = jnp.concatenate([value[:cut], value[cut:] + extra], axis=0)
        rs_buf[c, i] = value.astype(HALF)
        rs_copy(c, i).start()

    AG_TO = (2, -2, 1, -1, 2, 1, -1, -2)
    AG_FROM = (0, 0, 0, 0, -2, -2, 2, 2)
    AG_ROWS = (both, both, both, both, low, both, both, high)

    def ag_copy(c, i, arriving=False):
        origin = place(AG_FROM[i] - AG_TO[i]) if arriving else place(AG_FROM[i])
        piece = ag.at[c, origin, AG_ROWS[i], :]
        return remote(piece, piece, a_ss.at[c, i], a_rs.at[c, i], at_z(AG_TO[i]))

    def g_copies(k, c, slot):
        return [
            remote(grads.at[c, band(k), pl.ds(i * BLK, BLK)], ref.at[:, columns(slot, c)],
                   g_ss.at[c, i, k], g_rs.at[c, i, slot], at_y(k))
            for i, ref in enumerate((gate_out, up_out, down_out))
        ]

    def g_local(c):
        return [
            pltpu.make_async_copy(grads.at[c, band(y), pl.ds(i * BLK, BLK)], ref.at[:, columns(y, c)], own_s.at[c, i])
            for i, ref in enumerate((gate_out, up_out, down_out))
        ]

    def first(c):
        wait_all(w_local(c))
        others(ny, y, lambda k: recv_all(w_copies(k, c, k)))
        part[c, :, :, 0 : 2 * BLK] = contract(x_all(), wall[c, :, 0 : 2 * BLK], 1, 0).reshape(nz, group, 2 * BLK)
        part[c, :, :, 2 * BLK : 3 * BLK] = contract(dyb[...], wall[c, :, 2 * BLK : 3 * BLK], 1, 0).reshape(nz, group, BLK)
        rs_send(c, 0, 4)
        rs_send(c, 7, 4)
        rs_send(c, 1, 3)
        rs_send(c, 2, -3)
        rs_send(c, 5, -1)
        rs_send(c, 6, 1)

    def middle(c):
        if c == 0:
            others(ny, y, lambda k: wt_wait(k).wait_recv())
        total = part[c, z]
        for i in (5, 6, 4, 3):
            rs_copy(c, i).wait_recv()
            total = total + rs_recv[c, i].astype(FULL)
        gate_pre, up_pre, hidden_grad = total[:, :BLK], total[:, BLK : 2 * BLK], total[:, 2 * BLK :]
        weight = wbuf[:, :, c * BLK : (c + 1) * BLK].reshape(group, BLK)
        sigma = jax.nn.sigmoid(gate_pre)
        silu = gate_pre * sigma
        scaled = weight * hidden_grad
        ag[c, z, :, 0:BLK] = (scaled * up_pre * sigma * (1.0 + gate_pre * (1.0 - sigma))).astype(HALF)
        ag[c, z, :, BLK : 2 * BLK] = (scaled * silu).astype(HALF)
        ag[c, z, :, 2 * BLK : 3 * BLK] = (weight * silu * up_pre).astype(HALF)
        for i in range(4):
            ag_copy(c, i).start()

    def halves(c):
        pair = ag[c, :, :, 0 : 2 * BLK].reshape(tokens_all, 2 * BLK)
        return pair, ag[c, :, :, 2 * BLK : 3 * BLK].reshape(tokens_all, BLK)

    def block_grads(c):
        pair, hidden = halves(c)
        grads[c, :, 0 : 2 * BLK] = contract(xtr[...], pair, 1, 0).astype(HALF)
        grads[c, :, 2 * BLK : 3 * BLK] = contract(dytr[...], hidden, 1, 0).astype(HALF)
        others(ny, y, lambda k: start_all(g_copies(k, c, y)))
        start_all(g_local(c))

    def outputs(c):
        pair, hidden = halves(c)
        out_part = contract(hidden, wall[c, :, 2 * BLK : 3 * BLK], 1, 1)
        in_part = contract(pair, wall[c, :, 0 : 2 * BLK], 1, 1)
        if c > 0:
            out_part = out_part + acc[0]
            in_part = in_part + acc[1]
        if c < nc - 1:
            acc[0], acc[1] = out_part, in_part
        else:
            parts = jnp.concatenate([out_part, in_part], axis=1).reshape(nj, group, 2 * feats)
            op_send[...] = parts.astype(HALF)
            for k in sorted(range(1, nx), key=lambda k: -min(k, nx - k)):
                oc_copy(lax.rem(x_me + k, nx)).start()
            oc_copy(x_me).start()

    def oc_copy(k):
        return remote(op_send.at[slot_of(2 * k + 1 - core)], op_core.at[k], oc_ss.at[k], oc_rs.at[k], other_core)

    def op_copy(k, slot):
        return remote(op_buf.at[k], op_recv.at[slot], o_ss.at[k], o_rs.at[slot], at_x(k))

    def second(c):
        rs_send(c, 4, 2, 1, 7)
        rs_send(c, 3, -2, 2, 0)

    def onward(c):
        ag_copy(c, 0, True).wait_recv()
        ag_copy(c, 4).start()
        ag_copy(c, 5).start()
        ag_copy(c, 1, True).wait_recv()
        ag_copy(c, 6).start()
        ag_copy(c, 7).start()

    def arrived(c):
        for i in (2, 3, 5, 6, 4, 7):
            ag_copy(c, i, True).wait_recv()

    def turned():
        xtr[...] = x_all().T
        dytr[...] = dyb[...].T

    first(0)
    first(1)
    second(0)
    for c in range(2, nc):
        first(c)
    for c in range(1, nc):
        second(c)
    for c in range(nc):
        middle(c)
    turned()
    for c in range(nc):
        onward(c)
    for c in range(nc):
        arrived(c)
        if c < nc - 1:
            block_grads(c)
        outputs(c)
    block_grads(nc - 1)

    def pass_on(k):
        oc_copy(k).wait_recv()
        op_buf[k] = (op_send[slot_of(2 * k + core)].astype(FULL) + op_core[k].astype(FULL)).astype(HALF)
        op_copy(k, x_me).start()

    for k in sorted(range(1, nx), key=lambda k: -min(k, nx - k)):
        pass_on(lax.rem(x_me + k, nx))
    oc_copy(x_me).wait_recv()
    op_recv[x_me] = op_core[x_me]
    others(nx, x_me, lambda k: op_copy(k, k).wait_recv())
    summed = jnp.sum(op_recv[...].astype(FULL), axis=0) + op_send[mine].astype(FULL)
    t_send[...] = widen(
        jnp.concatenate(
            [summed[:, :feats].reshape(ny, 8, feats), summed[:, feats:].reshape(ny, 8, feats)], axis=1
        ),
        padded,
    )

    def t_copy(k):
        return remote(t_send.at[k], t_recv.at[y], t_ss.at[k], t_rs.at[y], at_source(k))

    def t_wait(k):
        return remote(t_send.at[k], t_recv.at[k], t_ss.at[k], t_rs.at[k], at_keeper(k))

    each_y(lambda k: t_copy(k).start())

    for c in range(nc):
        others(ny, y, lambda k: recv_all(g_copies(k, c, k)))
    each_y(lambda k: x_copy(k).wait_send())
    others(ny, y, lambda k: wt_copy(k).wait_send())
    others(nx, x_me, lambda k: xb_copy(k, mine).wait_send())
    for k in range(nx):
        xc_copy(k, core).wait_send()
        oc_copy(k).wait_send()
    others(nx, x_me, lambda k: op_copy(k, x_me).wait_send())
    for c in range(nc):
        others(ny, y, lambda k: send_all(w_copies(k, c, y)))
        for i in range(nz):
            rs_copy(c, i).wait_send()
            ag_copy(c, i).wait_send()
        others(ny, y, lambda k: send_all(g_copies(k, c, y)))
        wait_all(g_local(c))

    each_y(lambda k: t_wait(k).wait_recv())
    final = jnp.sum(t_recv[...].astype(FULL), axis=0)
    mixed_ref[...] = final[:8, :feats].astype(HALF)
    dtok_ref[...] = final[8:, :feats].astype(HALF)
    each_y(lambda k: t_copy(k).wait_send())


def finish(mixed_ref, dtok_ref, gate_ref, up_ref, down_ref, mixed_out, dtok_out, gate_out, up_out, down_out,
           small, halves, fulls, in_s, out_s):
    _, steps, _, width = halves.shape
    moved = [
        (pltpu.make_async_copy(source, small.at[i], in_s.at[i, 0]), pltpu.make_async_copy(small.at[i], target, out_s.at[i, 0]))
        for i, (source, target) in enumerate(((mixed_ref, mixed_out), (dtok_ref, dtok_out)))
    ]
    wide = [(gate_ref, gate_out), (up_ref, up_out), (down_ref, down_out)]

    def load(i, k):
        return pltpu.make_async_copy(wide[i][0].at[:, pl.ds(k * width, width)], halves.at[i, k], in_s.at[2 + i, k])

    def store(i, k):
        return pltpu.make_async_copy(fulls.at[i, k], wide[i][1].at[:, pl.ds(k * width, width)], out_s.at[2 + i, k])

    parts = [(i, k) for i in range(3) for k in range(steps)]
    for i, k in parts:
        load(i, k).start()
    for source, _ in moved:
        source.start()
    for i, k in parts:
        load(i, k).wait()
        fulls[i, k] = halves[i, k].astype(FULL)
        store(i, k).start()
    for source, target in moved:
        source.wait()
        target.start()
    for _, target in moved:
        target.wait()
    for i, k in parts:
        store(i, k).wait()


def shards(tokens, d_out, gate_dense, up_dense, down_dense, block_map, routes, route_gates):
    nj = lax.axis_size("dp")
    ny = lax.axis_size("expert") // nj
    nx = nj // 2
    per = block_map.shape[1] // nj
    rows, width = gate_dense.shape
    tok, feats = tokens.shape
    nc = width // BLK // ny
    group = tok * ny
    padded = -(-feats // BLK) * BLK
    dma = pltpu.SemaphoreType.DMA
    vmem = pl.BlockSpec(memory_space=pltpu.VMEM)
    hbm = pl.BlockSpec(memory_space=pltpu.HBM)
    outs = (
        jax.ShapeDtypeStruct((tok, feats), HALF),
        jax.ShapeDtypeStruct((tok, feats), HALF),
    ) + (jax.ShapeDtypeStruct((rows, width), HALF),) * 3
    results = pl.pallas_call(
        functools.partial(kernel, nj, ny, nc, per),
        out_shape=outs,
        in_specs=[hbm] * 8,
        out_specs=(vmem,) * 2 + (hbm,) * 3,
        scratch_shapes=[
            pltpu.VMEM((2 * tok, padded), HALF),
            pltpu.VMEM((ny, 2 * tok, padded), HALF),
            pltpu.VMEM((nj, group, 2 * feats), HALF),
            pltpu.VMEM((nj * group, feats), HALF),
            pltpu.VMEM((feats, nj * group), HALF),
            pltpu.VMEM((feats, nj * group), HALF),
            pltpu.VMEM((ny, tok, nc * BLK), FULL),
            pltpu.VMEM((ny, tok, nc * BLK), FULL),
            pltpu.VMEM((nc, ny * rows, 3 * BLK), HALF),
            pltpu.VMEM((nc, nj, group, 3 * BLK), FULL),
            pltpu.VMEM((nc, nj, group, 3 * BLK), HALF),
            pltpu.VMEM((nc, nj, group, 3 * BLK), HALF),
            pltpu.VMEM((nc, nj, group, 3 * BLK), HALF),
            pltpu.VMEM((nc, ny * rows, 3 * BLK), HALF),
            pltpu.VMEM((2, nj * group, feats), FULL),
            pltpu.VMEM((nj, group, 2 * feats), HALF),
            pltpu.VMEM((nx, group, 2 * feats), HALF),
            pltpu.VMEM((nx, group, 2 * feats), HALF),
            pltpu.VMEM((nx, group, 2 * feats), HALF),
            pltpu.VMEM((ny, 2 * tok, padded), HALF),
            pltpu.VMEM((ny, 2 * tok, padded), HALF),
            pltpu.VMEM((tok, feats), HALF),
            pltpu.VMEM((tok, feats), HALF),
            pltpu.VMEM(routes.shape, jnp.int32),
            pltpu.VMEM(block_map.shape[::-1], jnp.int32),
            pltpu.VMEM((1, routes.shape[1]), FULL),
            dma((5,)), dma((nc, 3)),
            dma((ny,)), dma((ny,)), dma((nx,)), dma((nj,)), dma((nx,)),
            dma((ny,)), dma((ny,)), dma((nc, 3)),
            dma((nc, 3, ny)), dma((nc, 3, ny)),
            dma((nc, nj)), dma((nc, nj)), dma((nc, nj)), dma((nc, nj)),
            dma((nc, 3, ny)), dma((nc, 3, ny)),
            dma((nx,)), dma((nx,)), dma((nx,)), dma((nx,)), dma((ny,)), dma((ny,)),
        ],
        compiler_params=pltpu.CompilerParams(
            collective_id=0, has_side_effects=True, vmem_limit_bytes=LIMIT
        ),
    )(tokens, d_out, routes, block_map.T, route_gates.reshape(1, -1), gate_dense, up_dense, down_dense.T)
    steps = 2
    mixed, d_tokens, gate_grad, up_grad, down_grad = pl.pallas_call(
        finish,
        out_shape=outs[:2] + (jax.ShapeDtypeStruct((rows, width), FULL),) * 3,
        in_specs=[hbm] * 5,
        out_specs=(hbm,) * 5,
        scratch_shapes=[
            pltpu.VMEM((2, tok, feats), HALF),
            pltpu.VMEM((3, steps, rows, width // steps), HALF),
            pltpu.VMEM((3, steps, rows, width // steps), FULL),
            dma((5, steps)),
            dma((5, steps)),
        ],
        compiler_params=pltpu.CompilerParams(vmem_limit_bytes=LIMIT),
    )(*results)
    return mixed, d_tokens, gate_grad, up_grad, down_grad.T


def solution(mesh):
    in_specs = (
        P("expert", "dp"),
        P("expert", "dp"),
        P("expert", "dp"),
        P("expert", "dp"),
        P("dp", "expert"),
        P(),
        P("expert", None),
        P(),
    )
    out_specs = (
        P("expert", "dp"),
        P("expert", "dp"),
        P("expert", "dp"),
        P("expert", "dp"),
        P("dp", "expert"),
    )
    return jax.shard_map(shards, mesh=mesh, in_specs=in_specs, out_specs=out_specs, check_vma=False)
```

```python
import functools

import jax
import jax.numpy as jnp
from jax import lax
from jax.experimental import pallas as pl
from jax.experimental.pallas import tpu as pltpu
from jax.sharding import PartitionSpec as P

BLK = 128
MESH = pl.DeviceIdType.MESH
LIMIT = 60 * 1024 * 1024
HALF, FULL = jnp.bfloat16, jnp.float32


def contract(left, right, left_dim, right_dim):
    return lax.dot_general(left, right, (((left_dim,), (right_dim,)), ((), ())), preferred_element_type=FULL)


def widen(rows, lanes):
    fill = jnp.zeros(rows.shape[:-1] + (lanes - rows.shape[-1],), rows.dtype)
    return jnp.concatenate([rows, fill], axis=-1).astype(HALF)


def kernel(
    nj, ny, nc, per,
    tok_hbm, cot_hbm, routes_hbm, map_hbm, gates_hbm, gate_ref, up_ref, down_ref,
    t_recv, gate_out, up_out, down_out,
    xs, xt, xb, dyb, xtr, dytr, wts, wbuf, wall, part, rs_buf, rs_recv, ag, grads, acc,
    op_send, op_core, op_buf, op_recv, t_send,
    tok_ref, cot_ref, routes_ref, map_ref, gates_ref, in_s, own_s,
    xt_ss, xt_rs, xb_ss, xb_rs, xc_ss, wt_ss, wt_rs, wl_s, w_ss, w_rs, r_ss, r_rs, a_ss, a_rs, g_ss, g_rs,
    oc_ss, oc_rs, o_ss, o_rs, t_ss, t_rs,
):
    nz, nx = nj, nj // 2
    j = lax.axis_index("dp")
    e = lax.axis_index("expert")
    x_me, core = j // 2, lax.rem(j, 2)
    z, y = e // ny, lax.rem(e, ny)
    rows = gate_ref.shape[0]
    quarter = gate_ref.shape[1] // ny
    feats, padded = tok_hbm.shape[1], xs.shape[1]
    group = 8 * ny
    tokens_all = nj * group

    def at_y(k):
        return (j, z * ny + k)

    def at_z(k):
        return (j, lax.rem(z + k + nz, nz) * ny + y)

    def at_x(k):
        return (2 * k + core, e)

    def pick(values, index):
        return sum(jnp.where(index == i, value, 0) for i, value in enumerate(values))

    def slot_of(device):
        ahead = lax.rem(device // 2 - z // 2 + nx, nx)
        return lax.rem(z + pick((4, 3, 5, 2, 1, 0, 6, 7), 2 * ahead + lax.rem(device, 2)), nz)

    mine = slot_of(j)
    ahead = lax.rem(z - j + nz, nz)
    keeper = 2 * lax.rem(j // 2 + pick((2, 2, 1, 0, 0, 1, 3, 3), ahead), nx) + pick((1, 0, 1, 1, 0, 0, 0, 1), ahead)

    def at_keeper(k):
        return (keeper, j * ny + k)

    def at_source(k):
        return (z, mine * ny + k)

    other_core = (2 * x_me + 1 - core, e)

    def others(n, me, body):
        for i in sorted(range(1, n), key=lambda i: -min(i, n - i)):
            body(lax.rem(me + i, n))

    def each_y(body):
        def step(k, _):
            body(k)
            return 0

        lax.fori_loop(0, ny, step, 0)

    def remote(src, dst, ss, rs, device):
        return pltpu.make_async_remote_copy(
            src_ref=src, dst_ref=dst, send_sem=ss, recv_sem=rs, device_id=device, device_id_type=MESH
        )

    small = [
        pltpu.make_async_copy(source, target, in_s.at[i])
        for i, (source, target) in enumerate(
            ((tok_hbm, tok_ref), (cot_hbm, cot_ref), (routes_hbm, routes_ref), (map_hbm, map_ref), (gates_hbm, gates_ref))
        )
    ]
    for copy in small:
        copy.start()

    barrier = pltpu.get_barrier_semaphore()

    def greet(device):
        pl.semaphore_signal(barrier, inc=1, device_id=device, device_id_type=MESH)

    each_y(lambda k: greet(at_keeper(k)))
    each_y(lambda k: greet(at_source(k)))
    others(ny, y, lambda k: greet(at_y(k)))
    for k in (2, -2, 1, -1):
        greet(at_z(k))
    others(nx, x_me, lambda k: greet(at_x(k)))
    greet(other_core)
    count = 2 * ny + (ny - 1) + 4 + (nx - 1) + 1

    for copy in small:
        copy.wait()
    xs[...] = widen(jnp.concatenate([tok_ref[...].astype(FULL), cot_ref[...].astype(FULL)], axis=0), padded)

    pl.semaphore_wait(barrier, count)

    def x_copy(k):
        return remote(xs, xt.at[y], xt_ss.at[k], xt_rs.at[y], at_keeper(k))

    def x_wait(k):
        return remote(xs, xt.at[k], xt_ss.at[k], xt_rs.at[k], at_source(k))

    each_y(lambda k: x_copy(k).start())

    def columns(k, c):
        return pl.ds(pl.multiple_of(k * quarter + c * BLK, BLK), BLK)

    def band(k):
        return pl.ds(pl.multiple_of(k * rows, 16), rows)

    def w_copies(k, c, slot):
        return [
            remote(ref.at[:, columns(k, c)], wall.at[c, band(slot), pl.ds(i * BLK, BLK)],
                   w_ss.at[c, i, k], w_rs.at[c, i, slot], at_y(k))
            for i, ref in enumerate((gate_ref, up_ref, down_ref))
        ]

    def w_local(c):
        return [
            pltpu.make_async_copy(ref.at[:, columns(y, c)], wall.at[c, band(y), pl.ds(i * BLK, BLK)], wl_s.at[c, i])
            for i, ref in enumerate((gate_ref, up_ref, down_ref))
        ]

    def start_all(copies):
        for copy in copies:
            copy.start()

    def wait_all(copies):
        for copy in copies:
            copy.wait()

    def recv_all(copies):
        for copy in copies:
            copy.wait_recv()

    def send_all(copies):
        for copy in copies:
            copy.wait_send()

    experts = map_ref.shape[1]
    names = lax.broadcasted_iota(jnp.int32, (8, experts), 1)
    named = jnp.zeros((8, experts), FULL)
    for k in range(routes_ref.shape[1]):
        named = named + jnp.where(routes_ref[:, k : k + 1] == names, gates_ref[:, k : k + 1], 0.0)
    picks = [map_ref[pl.ds(j * per + q, 1), :] - j * (ny * nc) for q in range(per)]
    for k in range(ny):
        for c in range(nc):
            takes = sum((pick == k * nc + c).astype(FULL) for pick in picks)
            weight = jnp.sum(named * takes, axis=1, keepdims=True)
            wts[k, :, c * BLK : (c + 1) * BLK] = jnp.broadcast_to(weight, (8, BLK))

    def wt_copy(k):
        return remote(wts.at[k], wbuf.at[y], wt_ss.at[k], wt_rs.at[y], at_y(k))

    def wt_wait(k):
        return remote(wts.at[k], wbuf.at[k], wt_ss.at[k], wt_rs.at[k], at_y(k))

    others(ny, y, lambda k: wt_copy(k).start())
    wbuf[y] = wts[y]

    others(ny, y, lambda k: start_all(w_copies(k, 0, y)))

    each_y(lambda k: x_wait(k).wait_recv())
    landed = xt[...].astype(FULL)[:, :, :feats]
    xb[mine] = jnp.concatenate(
        [landed[:, :8].reshape(group, feats), landed[:, 8:].reshape(group, feats)], axis=1
    ).astype(HALF)

    def xb_copy(k, slot):
        return remote(xb.at[slot], xb.at[slot], xb_ss.at[k], xb_rs.at[slot], at_x(k))

    def xc_copy(k, side):
        slot = slot_of(2 * k + side)
        return remote(xb.at[slot], xb.at[slot], xc_ss.at[k], xb_rs.at[slot], other_core)

    others(nx, x_me, lambda k: xb_copy(k, mine).start())
    xc_copy(x_me, core).start()
    for c in range(1, nc):
        others(ny, y, lambda k: start_all(w_copies(k, c, y)))
    for c in range(nc):
        start_all(w_local(c))

    def forward(k):
        xb_copy(k, slot_of(2 * k + core)).wait_recv()
        xc_copy(k, core).start()

    for k in sorted(range(1, nx), key=lambda k: min(k, nx - k)):
        forward(lax.rem(x_me + k, nx))

    def from_core(k, _):
        xc_copy(k, 1 - core).wait_recv()
        return 0

    lax.fori_loop(0, nx, from_core, 0)
    dyb[...] = xb[:, :, feats:].reshape(tokens_all, feats)

    def x_all():
        return xb[:, :, :feats].reshape(tokens_all, feats)

    def place(k):
        return lax.rem(z + k + nz, nz)

    cut = group // 2
    low, high, both = pl.ds(0, cut), pl.ds(cut, cut), pl.ds(0, group)
    RS_TO = (-2, 1, -1, -2, 2, -1, 1, 2)
    RS_ROWS = (low, both, both, both, both, both, both, high)

    def rs_copy(c, i):
        return remote(rs_buf.at[c, i, RS_ROWS[i], :], rs_recv.at[c, i, RS_ROWS[i], :],
                      r_ss.at[c, i], r_rs.at[c, i], at_z(RS_TO[i]))

    def rs_send(c, i, target, piece=None, half=None):
        value = part[c, place(target)]
        if piece is not None:
            rs_copy(c, half).wait_recv()
            rs_copy(c, piece).wait_recv()
            value = value + rs_recv[c, piece].astype(FULL)
            extra = rs_recv[c, half, RS_ROWS[half], :].astype(FULL)
            if half == 0:
                value = jnp.concatenate([value[:cut] + extra, value[cut:]], axis=0)
            else:
                value = jnp.concatenate([value[:cut], value[cut:] + extra], axis=0)
        rs_buf[c, i] = value.astype(HALF)
        rs_copy(c, i).start()

    AG_TO = (2, -2, 1, -1, 2, 1, -1, -2)
    AG_FROM = (0, 0, 0, 0, -2, -2, 2, 2)
    AG_ROWS = (both, both, both, both, low, both, both, high)

    def ag_copy(c, i, arriving=False):
        origin = place(AG_FROM[i] - AG_TO[i]) if arriving else place(AG_FROM[i])
        piece = ag.at[c, origin, AG_ROWS[i], :]
        return remote(piece, piece, a_ss.at[c, i], a_rs.at[c, i], at_z(AG_TO[i]))

    def g_copies(k, c, slot):
        return [
            remote(grads.at[c, band(k), pl.ds(i * BLK, BLK)], ref.at[:, columns(slot, c)],
                   g_ss.at[c, i, k], g_rs.at[c, i, slot], at_y(k))
            for i, ref in enumerate((gate_out, up_out, down_out))
        ]

    def g_local(c):
        return [
            pltpu.make_async_copy(grads.at[c, band(y), pl.ds(i * BLK, BLK)], ref.at[:, columns(y, c)], own_s.at[c, i])
            for i, ref in enumerate((gate_out, up_out, down_out))
        ]

    def first(c):
        wait_all(w_local(c))
        others(ny, y, lambda k: recv_all(w_copies(k, c, k)))
        part[c, :, :, 0 : 2 * BLK] = contract(x_all(), wall[c, :, 0 : 2 * BLK], 1, 0).reshape(nz, group, 2 * BLK)
        part[c, :, :, 2 * BLK : 3 * BLK] = contract(dyb[...], wall[c, :, 2 * BLK : 3 * BLK], 1, 0).reshape(nz, group, BLK)
        rs_send(c, 0, 4)
        rs_send(c, 7, 4)
        rs_send(c, 1, 3)
        rs_send(c, 2, -3)
        rs_send(c, 5, -1)
        rs_send(c, 6, 1)

    def middle(c):
        if c == 0:
            others(ny, y, lambda k: wt_wait(k).wait_recv())
        total = part[c, z]
        for i in (5, 6, 4, 3):
            rs_copy(c, i).wait_recv()
            total = total + rs_recv[c, i].astype(FULL)
        gate_pre, up_pre, hidden_grad = total[:, :BLK], total[:, BLK : 2 * BLK], total[:, 2 * BLK :]
        weight = wbuf[:, :, c * BLK : (c + 1) * BLK].reshape(group, BLK)
        sigma = jax.nn.sigmoid(gate_pre)
        silu = gate_pre * sigma
        scaled = weight * hidden_grad
        ag[c, z, :, 0:BLK] = (scaled * up_pre * sigma * (1.0 + gate_pre * (1.0 - sigma))).astype(HALF)
        ag[c, z, :, BLK : 2 * BLK] = (scaled * silu).astype(HALF)
        ag[c, z, :, 2 * BLK : 3 * BLK] = (weight * silu * up_pre).astype(HALF)
        for i in range(4):
            ag_copy(c, i).start()

    def halves(c):
        pair = ag[c, :, :, 0 : 2 * BLK].reshape(tokens_all, 2 * BLK)
        return pair, ag[c, :, :, 2 * BLK : 3 * BLK].reshape(tokens_all, BLK)

    def block_grads(c):
        pair, hidden = halves(c)
        grads[c, :, 0 : 2 * BLK] = contract(xtr[...], pair, 1, 0).astype(HALF)
        grads[c, :, 2 * BLK : 3 * BLK] = contract(dytr[...], hidden, 1, 0).astype(HALF)
        others(ny, y, lambda k: start_all(g_copies(k, c, y)))
        start_all(g_local(c))

    def outputs(c):
        pair, hidden = halves(c)
        out_part = contract(hidden, wall[c, :, 2 * BLK : 3 * BLK], 1, 1)
        in_part = contract(pair, wall[c, :, 0 : 2 * BLK], 1, 1)
        if c > 0:
            out_part = out_part + acc[0]
            in_part = in_part + acc[1]
        if c < nc - 1:
            acc[0], acc[1] = out_part, in_part
        else:
            parts = jnp.concatenate([out_part, in_part], axis=1).reshape(nj, group, 2 * feats)
            op_send[...] = parts.astype(HALF)
            for k in sorted(range(1, nx), key=lambda k: -min(k, nx - k)):
                oc_copy(lax.rem(x_me + k, nx)).start()
            oc_copy(x_me).start()

    def oc_copy(k):
        return remote(op_send.at[slot_of(2 * k + 1 - core)], op_core.at[k], oc_ss.at[k], oc_rs.at[k], other_core)

    def op_copy(k, slot):
        return remote(op_buf.at[k], op_recv.at[slot], o_ss.at[k], o_rs.at[slot], at_x(k))

    def second(c):
        rs_send(c, 4, 2, 1, 7)
        rs_send(c, 3, -2, 2, 0)

    def onward(c):
        ag_copy(c, 0, True).wait_recv()
        ag_copy(c, 4).start()
        ag_copy(c, 5).start()
        ag_copy(c, 1, True).wait_recv()
        ag_copy(c, 6).start()
        ag_copy(c, 7).start()

    def arrived(c):
        for i in (2, 3, 5, 6, 4, 7):
            ag_copy(c, i, True).wait_recv()

    def turned():
        xtr[...] = x_all().T
        dytr[...] = dyb[...].T

    first(0)
    first(1)
    second(0)
    for c in range(2, nc):
        first(c)
    for c in range(1, nc):
        second(c)
    for c in range(nc):
        middle(c)
    turned()
    for c in range(nc):
        onward(c)
    for c in range(nc):
        arrived(c)
        if c < nc - 1:
            block_grads(c)
        outputs(c)
    block_grads(nc - 1)

    def pass_on(k):
        oc_copy(k).wait_recv()
        op_buf[k] = (op_send[slot_of(2 * k + core)].astype(FULL) + op_core[k].astype(FULL)).astype(HALF)
        op_copy(k, x_me).start()

    for k in sorted(range(1, nx), key=lambda k: -min(k, nx - k)):
        pass_on(lax.rem(x_me + k, nx))
    oc_copy(x_me).wait_recv()
    op_recv[x_me] = op_core[x_me]
    others(nx, x_me, lambda k: op_copy(k, k).wait_recv())
    summed = jnp.sum(op_recv[...].astype(FULL), axis=0) + op_send[mine].astype(FULL)
    t_send[...] = widen(
        jnp.concatenate(
            [summed[:, :feats].reshape(ny, 8, feats), summed[:, feats:].reshape(ny, 8, feats)], axis=1
        ),
        padded,
    )

    def t_copy(k):
        return remote(t_send.at[k], t_recv.at[y], t_ss.at[k], t_rs.at[y], at_source(k))

    def t_wait(k):
        return remote(t_send.at[k], t_recv.at[k], t_ss.at[k], t_rs.at[k], at_keeper(k))

    each_y(lambda k: t_copy(k).start())

    for c in range(nc):
        others(ny, y, lambda k: recv_all(g_copies(k, c, k)))
    each_y(lambda k: x_copy(k).wait_send())
    others(ny, y, lambda k: wt_copy(k).wait_send())
    others(nx, x_me, lambda k: xb_copy(k, mine).wait_send())
    for k in range(nx):
        xc_copy(k, core).wait_send()
        oc_copy(k).wait_send()
    others(nx, x_me, lambda k: op_copy(k, x_me).wait_send())
    for c in range(nc):
        others(ny, y, lambda k: send_all(w_copies(k, c, y)))
        for i in range(nz):
            rs_copy(c, i).wait_send()
            ag_copy(c, i).wait_send()
        others(ny, y, lambda k: send_all(g_copies(k, c, y)))
        wait_all(g_local(c))

    each_y(lambda k: t_wait(k).wait_recv())
    each_y(lambda k: t_copy(k).wait_send())


def finish(parts_ref, gate_ref, up_ref, down_ref, mixed_out, dtok_out, gate_out, up_out, down_out,
           pieces, small, halves, fulls, in_s, out_s):
    _, steps, _, width = halves.shape
    _, tok, feats = small.shape
    arrive = pltpu.make_async_copy(parts_ref, pieces, in_s.at[0, 0])
    leave = [
        pltpu.make_async_copy(small.at[i], target, out_s.at[i, 0]) for i, target in enumerate((mixed_out, dtok_out))
    ]
    wide = [(gate_ref, gate_out), (up_ref, up_out), (down_ref, down_out)]

    def load(i, k):
        return pltpu.make_async_copy(wide[i][0].at[:, pl.ds(k * width, width)], halves.at[i, k], in_s.at[2 + i, k])

    def store(i, k):
        return pltpu.make_async_copy(fulls.at[i, k], wide[i][1].at[:, pl.ds(k * width, width)], out_s.at[2 + i, k])

    arrive.start()
    parts = [(i, k) for i in range(3) for k in range(steps)]
    for i, k in parts:
        load(i, k).start()
    arrive.wait()
    final = jnp.sum(pieces[...].astype(FULL), axis=0)
    for i in range(2):
        small[i] = final[i * tok : (i + 1) * tok, :feats].astype(HALF)
        leave[i].start()
    for i, k in parts:
        load(i, k).wait()
        fulls[i, k] = halves[i, k].astype(FULL)
        store(i, k).start()
    for copy in leave:
        copy.wait()
    for i, k in parts:
        store(i, k).wait()


def shards(tokens, d_out, gate_dense, up_dense, down_dense, block_map, routes, route_gates):
    nj = lax.axis_size("dp")
    ny = lax.axis_size("expert") // nj
    nx = nj // 2
    per = block_map.shape[1] // nj
    rows, width = gate_dense.shape
    tok, feats = tokens.shape
    nc = width // BLK // ny
    group = tok * ny
    padded = -(-feats // BLK) * BLK
    dma = pltpu.SemaphoreType.DMA
    hbm = pl.BlockSpec(memory_space=pltpu.HBM)
    outs = (jax.ShapeDtypeStruct((ny, 2 * tok, padded), HALF),) + (jax.ShapeDtypeStruct((rows, width), HALF),) * 3
    results = pl.pallas_call(
        functools.partial(kernel, nj, ny, nc, per),
        out_shape=outs,
        in_specs=[hbm] * 8,
        out_specs=(hbm,) * 4,
        scratch_shapes=[
            pltpu.VMEM((2 * tok, padded), HALF),
            pltpu.VMEM((ny, 2 * tok, padded), HALF),
            pltpu.VMEM((nj, group, 2 * feats), HALF),
            pltpu.VMEM((nj * group, feats), HALF),
            pltpu.VMEM((feats, nj * group), HALF),
            pltpu.VMEM((feats, nj * group), HALF),
            pltpu.VMEM((ny, tok, nc * BLK), FULL),
            pltpu.VMEM((ny, tok, nc * BLK), FULL),
            pltpu.VMEM((nc, ny * rows, 3 * BLK), HALF),
            pltpu.VMEM((nc, nj, group, 3 * BLK), FULL),
            pltpu.VMEM((nc, nj, group, 3 * BLK), HALF),
            pltpu.VMEM((nc, nj, group, 3 * BLK), HALF),
            pltpu.VMEM((nc, nj, group, 3 * BLK), HALF),
            pltpu.VMEM((nc, ny * rows, 3 * BLK), HALF),
            pltpu.VMEM((2, nj * group, feats), FULL),
            pltpu.VMEM((nj, group, 2 * feats), HALF),
            pltpu.VMEM((nx, group, 2 * feats), HALF),
            pltpu.VMEM((nx, group, 2 * feats), HALF),
            pltpu.VMEM((nx, group, 2 * feats), HALF),
            pltpu.VMEM((ny, 2 * tok, padded), HALF),
            pltpu.VMEM((tok, feats), HALF),
            pltpu.VMEM((tok, feats), HALF),
            pltpu.VMEM(routes.shape, jnp.int32),
            pltpu.VMEM(block_map.shape[::-1], jnp.int32),
            pltpu.VMEM((1, routes.shape[1]), FULL),
            dma((5,)), dma((nc, 3)),
            dma((ny,)), dma((ny,)), dma((nx,)), dma((nj,)), dma((nx,)),
            dma((ny,)), dma((ny,)), dma((nc, 3)),
            dma((nc, 3, ny)), dma((nc, 3, ny)),
            dma((nc, nj)), dma((nc, nj)), dma((nc, nj)), dma((nc, nj)),
            dma((nc, 3, ny)), dma((nc, 3, ny)),
            dma((nx,)), dma((nx,)), dma((nx,)), dma((nx,)), dma((ny,)), dma((ny,)),
        ],
        compiler_params=pltpu.CompilerParams(
            collective_id=0, has_side_effects=True, vmem_limit_bytes=LIMIT
        ),
    )(tokens, d_out, routes, block_map.T, route_gates.reshape(1, -1), gate_dense, up_dense, down_dense.T)
    steps = 2
    mixed, d_tokens, gate_grad, up_grad, down_grad = pl.pallas_call(
        finish,
        out_shape=(jax.ShapeDtypeStruct((tok, feats), HALF),) * 2 + (jax.ShapeDtypeStruct((rows, width), FULL),) * 3,
        in_specs=[hbm] * 4,
        out_specs=(hbm,) * 5,
        scratch_shapes=[
            pltpu.VMEM((ny, 2 * tok, padded), HALF),
            pltpu.VMEM((2, tok, feats), HALF),
            pltpu.VMEM((3, steps, rows, width // steps), HALF),
            pltpu.VMEM((3, steps, rows, width // steps), FULL),
            dma((5, steps)),
            dma((5, steps)),
        ],
        compiler_params=pltpu.CompilerParams(vmem_limit_bytes=LIMIT),
    )(*results)
    return mixed, d_tokens, gate_grad, up_grad, down_grad.T


def solution(mesh):
    in_specs = (
        P("expert", "dp"),
        P("expert", "dp"),
        P("expert", "dp"),
        P("expert", "dp"),
        P("dp", "expert"),
        P(),
        P("expert", None),
        P(),
    )
    out_specs = (
        P("expert", "dp"),
        P("expert", "dp"),
        P("expert", "dp"),
        P("expert", "dp"),
        P("dp", "expert"),
    )
    return jax.shard_map(shards, mesh=mesh, in_specs=in_specs, out_specs=out_specs, check_vma=False)
```
